32 devices in a mesh: dp: 16 (over z, y, core), mp: 2 (over x).
Axes of the slice: x: 2, y: 2, z: 4, core: 2. Of those that a mesh axis runs over, the one named last changes fastest.
Arguments:
- tokens: bfloat16 [8192, 768], P(('dp', 'mp')), may hold values from -6 to 6
- cotangent: bfloat16 [8192, 768], P(('dp', 'mp')), may hold values from -6 to 6
- lengths: int32 [32, 8], P(('dp', 'mp')), may hold values from 1 to 202, 256 in all within a row
- random_proj: float32 [2, 12, 64, 32], replicated, may hold values from -5 to 5
- attn_weight: bfloat16 [2, 3, 768, 768], P(None, None, None, 'mp'), may hold values from -0.21875 to 0.21875
- attn_bias: bfloat16 [2, 3, 768], P(None, None, 'mp'), may hold values from -1 to 1
- out_weight: bfloat16 [2, 768, 768], P(None, 'mp'), may hold values from -0.875 to 0.875
- norm_gains: bfloat16 [2, 2, 768], replicated, may hold values from 0.5 to 1.5
- biases: bfloat16 [2, 4, 768], replicated, may hold values from -1 to 1
- up_weight: bfloat16 [2, 768, 3072], P(None, None, 'mp'), may hold values from -0.21875 to 0.21875
- up_bias: bfloat16 [2, 3072], P(None, 'mp'), may hold values from -1 to 1
- down_weight: bfloat16 [2, 3072, 768], P(None, 'mp'), may hold values from -0.109375 to 0.109375
Outputs:
- stack_out: bfloat16 [8192, 768], P(('dp', 'mp'))
- tokens_grad: float32 [8192, 768], P(('dp', 'mp'))
- attn_weight_grad: float32 [2, 3, 768, 768], P(None, None, None, 'mp')
- attn_bias_grad: float32 [2, 3, 768], P(None, None, 'mp')
- out_weight_grad: float32 [2, 768, 768], P(None, 'mp')
- norm_gains_grad: float32 [2, 2, 768], P(None, None, 'mp')
- biases_grad: float32 [2, 4, 768], P(None, None, 'mp')
- up_weight_grad: float32 [2, 768, 3072], P(None, None, 'mp')
- up_bias_grad: float32 [2, 3072], P(None, 'mp')
- down_weight_grad: float32 [2, 3072, 768], P(None, 'mp')
The draws below stay inside these ranges and needn't reach their ends.
Inputs may be any that keep to these rules, and one draw needn't show every extreme that they name: `lengths`: each row sums to 256 and its largest entry is 202.
All inputs are finite; a program needn't handle non-finite values.
Results may differ from the reference program's by a relative error of at most 0.012.
Values may be sent and summed in bfloat16 or wider, within the bound.
A program may use at most 256 MiB of HBM per device.

```python
import math
import jax
import jax.numpy as jnp
import numpy as np
from jax import lax

D = 768
HEADS = 12
HD = 64
FEATS = 32
FF = 3072
LAYERS = 2
TOK_DEV = 256
MOST = 202
MOLS = 8
BLOCKS = 32
TOKENS = 8192


def level_of(key, dims, cuts, smallest, high):
    def one(dim, blocks):
        steps = jax.random.uniform(jax.random.fold_in(jax.random.fold_in(key, 6), dim), (blocks,), jnp.float32, smallest / len(cuts), high / len(cuts))
        return jnp.repeat(jnp.exp(steps), dims[dim] // blocks).reshape((-1,) + (1,) * (len(dims) - dim - 1))

    loudness = one(*cuts[0])
    for cut in cuts[1:]:
        loudness = loudness * one(*cut)
    return loudness


def profile(amount, total, reach, slope):
    weights = [(1 << 20) // math.isqrt(rank ** slope) + 1 for rank in range(2, amount + 1)]
    rest, counts = total - reach - (amount - 1), [1] * (amount - 1)
    while rest > 0:
        candidates = [i for i in range(amount - 1) if counts[i] < reach]
        mass, budget = sum([weights[i] for i in candidates]), rest
        for i in candidates:
            more = min(reach - counts[i], max(1, budget * weights[i] // mass), rest)
            counts[i] = counts[i] + more
            rest = rest - more
    return np.array([reach] + counts)


def ragged(own_key, count, total, reach, lean):
    if count == 2:
        one = jax.random.randint(own_key, (), max(1, total - reach), min(reach, total - 1) + 1)
        return jnp.stack([one, total - one])
    tallies = jnp.asarray(profile(count, total, reach, lean), jnp.int32)
    twos = (count - 1) // 2
    source_of, sink = tallies[1:1 + 2 * twos:2], tallies[2:2 + 2 * twos:2]
    margin = jnp.minimum(source_of - 1, reach - sink)
    shifted = jax.random.randint(jax.random.fold_in(own_key, 1), (twos,), 0, 1 << 20) % (margin + 1)
    tallies = tallies.at[1:1 + 2 * twos:2].set(source_of - shifted).at[2:2 + 2 * twos:2].set(sink + shifted)
    return tallies[jax.random.permutation(jax.random.fold_in(own_key, 2), count)]


def noise(rng, shape, deviation, bound, shards=(), kind=jnp.bfloat16):
    drawn = deviation * jax.random.normal(rng, shape, jnp.float32)
    if shards:
        drawn = drawn * level_of(rng, shape, shards, -0.22, 0.18)
    return jnp.clip(drawn, -bound, bound).astype(kind)


def setup_inputs(seed: int = 0) -> dict:
    key_list = jax.random.split(jax.random.key(seed), 13)
    return {
        "tokens": noise(key_list[0], (TOKENS, D), 1.0, 6.0, ((0, 32),)),
        "cotangent": noise(key_list[1], (TOKENS, D), 1.0, 6.0, ((0, 32),)),
        "lengths": jax.vmap(lambda own: ragged(own, MOLS, TOK_DEV, MOST, 2))(jax.random.split(key_list[2], BLOCKS)).reshape((BLOCKS, MOLS)).astype(jnp.int32),
        "random_proj": noise(key_list[3], (LAYERS, HEADS, HD, FEATS), 1.0, 5.0, (), jnp.float32),
        "attn_weight": noise(key_list[4], (LAYERS, 3, D, D), D ** -0.5, 0.21875, ((3, 2),)),
        "attn_bias": noise(key_list[5], (LAYERS, 3, D), 0.2, 1.0, ((2, 2),)),
        "out_weight": noise(key_list[6], (LAYERS, D, D), (D // 16) ** -0.5, 0.875, ((1, 2),)),
        "norm_gains": jnp.clip(1.0 + 0.1 * jax.random.normal(key_list[7], (LAYERS, 2, D), jnp.float32), 0.5, 1.5).astype(jnp.bfloat16),
        "biases": noise(key_list[8], (LAYERS, 4, D), 0.2, 1.0),
        "up_weight": noise(key_list[9], (LAYERS, D, FF), D ** -0.5, 0.21875, ((2, 2),)),
        "up_bias": noise(key_list[10], (LAYERS, FF), 0.2, 1.0, ((1, 2),)),
        "down_weight": noise(key_list[11], (LAYERS, FF, D), FF ** -0.5, 0.109375, ((1, 2),)),
    }


highest = lax.Precision.HIGHEST

@jax.custom_vjp
def low(v):
    return lax.optimization_barrier(v.astype(jnp.bfloat16)).astype(jnp.float32)

@jax.custom_vjp
def low_back(v):
    return v

def low_keep(v):
    return (low(v), None)

def low_pass(kept, grad):
    return (grad,)

def back_keep(v):
    return (v, None)

def back_low(kept, grad):
    return (low(grad),)
low.defvjp(low_keep, low_pass)
low_back.defvjp(back_keep, back_low)

def layer_norm(values, scaling, shifting):
    average = lax.optimization_barrier(jnp.mean(values, axis=-1, keepdims=True))
    centred = values - average
    spread = lax.optimization_barrier(jnp.mean(centred * centred, axis=-1, keepdims=True))
    return centred * lax.rsqrt(spread + 1e-05) * scaling + shifting

def positions(lengths_row, row_count, head_size):
    finish = jnp.cumsum(lengths_row, dtype=jnp.int32)
    counter = jnp.arange(row_count, dtype=jnp.int32)
    passed = counter[:, None] >= finish[None, :]
    segment = lax.optimization_barrier(jnp.sum(passed.astype(jnp.int32), axis=1, dtype=jnp.int32))
    start_at = lax.optimization_barrier(jnp.sum(jnp.where(passed, lengths_row[None, :], 0), axis=1, dtype=jnp.int32))
    offset = (counter - start_at).astype(jnp.float32)
    half_size = head_size // 2
    frequency = jnp.exp(jnp.arange(half_size, dtype=jnp.float32) * (-2.0 * math.log(10000.0) / head_size))
    angles = offset[:, None] * frequency[None, :]
    same_mol = (segment[:, None] == segment[None, :]).astype(jnp.float32)
    return (jnp.cos(angles)[:, None, :], jnp.sin(angles)[:, None, :], same_mol)

def rotate(vectors, cosines, sines):
    half_size = vectors.shape[-1] // 2
    leading = vectors[..., :half_size]
    trailing = vectors[..., half_size:]
    return jnp.concatenate([leading * cosines - trailing * sines, trailing * cosines + leading * sines], axis=-1)

def features(vectors, random_proj):
    scaled = vectors * vectors.shape[-1] ** (-0.25)
    return jax.nn.softplus(jnp.einsum('thd,hdm->thm', scaled, random_proj, precision=highest))

def attend(queries, key_rows, values, random_proj, cosines, sines, same_mol):
    row_count, model_width = queries.shape
    head_count, head_size = (random_proj.shape[0], random_proj.shape[1])
    shaped = (row_count, head_count, head_size)
    query_feats = features(rotate(queries.reshape(shaped), cosines, sines), random_proj)
    key_feats = features(rotate(key_rows.reshape(shaped), cosines, sines), random_proj)
    scores = jnp.einsum('thm,shm->hts', query_feats, key_feats, precision=highest) * same_mol[None]
    numerator = jnp.einsum('hts,shd->thd', scores, values.reshape(shaped), precision=highest)
    denominator = lax.optimization_barrier(jnp.sum(scores, axis=2)).T[:, :, None]
    return (numerator / denominator).reshape(row_count, model_width)

def stack_forward(inputs, params, random_proj, lengths_row):
    attn_weight, attn_bias, out_weight, norm_gains, biases, up_weight, up_bias, down_weight = params
    cosines, sines, same_mol = positions(lengths_row, inputs.shape[0], random_proj.shape[2])
    current = inputs
    for layer_index in range(attn_weight.shape[0]):
        normed = low(layer_norm(current, norm_gains[layer_index, 0], biases[layer_index, 0]))
        triple = [low_back(jnp.dot(normed, attn_weight[layer_index, member], precision=highest) + attn_bias[layer_index, member]) for member in range(3)]
        context = low(attend(triple[0], triple[1], triple[2], random_proj[layer_index], cosines, sines, same_mol))
        middle = current + low_back(jnp.dot(context, out_weight[layer_index], precision=highest) + biases[layer_index, 1])
        second = low(layer_norm(middle, norm_gains[layer_index, 1], biases[layer_index, 2]))
        hidden = low_back(jnp.dot(second, up_weight[layer_index], precision=highest) + up_bias[layer_index])
        active = low(jax.nn.gelu(hidden, approximate=False))
        current = middle + low_back(jnp.dot(active, down_weight[layer_index], precision=highest) + biases[layer_index, 3])
    return current

def reference(tokens, cotangent, lengths, random_proj, attn_weight, attn_bias, out_weight, norm_gains, biases, up_weight, up_bias, down_weight):
    params = tuple((weight_in.astype(jnp.float32) for weight_in in (attn_weight, attn_bias, out_weight, norm_gains, biases, up_weight, up_bias, down_weight)))
    model_width = tokens.shape[1]
    inputs = tokens.astype(jnp.float32).reshape(BLOCKS, TOK_DEV, model_width)
    grads_in = cotangent.astype(jnp.float32).reshape(BLOCKS, TOK_DEV, model_width)

    def block_step(running, packed):
        block_in, block_grad, lengths_row = packed

        def run_stack(values, *weights):
            return stack_forward(values, weights, random_proj, lengths_row)
        result, pullback = jax.vjp(run_stack, block_in, *params)
        pulled = pullback(block_grad)
        running = tuple((earlier + grad_part for earlier, grad_part in zip(running, pulled[1:])))
        return (running, (result, pulled[0]))
    start_sums = tuple((jnp.zeros(weight_in.shape, jnp.float32) for weight_in in params))
    totals, (results, input_grads) = lax.scan(block_step, start_sums, (inputs, grads_in, lengths))
    return (results.reshape(TOKENS, model_width).astype(jnp.bfloat16), input_grads.reshape(TOKENS, model_width), totals[0], totals[1], totals[2], totals[3], totals[4], totals[5], totals[6], totals[7])
```

```python
import functools
import math

import jax
import jax.numpy as jnp
from jax import lax
from jax.experimental import pallas as pl
from jax.experimental.pallas import tpu as pltpu
from jax.sharding import PartitionSpec as P

MESH = pl.DeviceIdType.MESH
W = 384


def rdma(src, dst, send, recv, dev):
    return pltpu.make_async_remote_copy(
        src_ref=src, dst_ref=dst, send_sem=send, recv_sem=recv, device_id=dev, device_id_type=MESH
    )


def greet(peers):
    barrier = pltpu.get_barrier_semaphore()
    for peer in peers:
        pl.semaphore_signal(barrier, inc=1, device_id=peer, device_id_type=MESH)
    pl.semaphore_wait(barrier, len(peers))


def gather_kernel(spread, *refs):
    count = len(spread)
    small_in, ins = refs[0], refs[1 : 1 + count]
    small_out, outs = refs[1 + count], refs[2 + count : 2 + 2 * count]
    sends, recvs = refs[2 + 2 * count :]
    d, x = lax.axis_index("dp"), lax.axis_index("mp")
    core, yy, zz = d % 2, (d // 2) % 2, (d // 4) % 2
    to_x = (d, 1 - x)
    to_core = (d + 1 - 2 * core, x)
    to_y = (d + 2 - 4 * yy, x)
    to_z = (d + 4 - 8 * zz, x)
    greet([to_x, to_core, to_y, to_z])
    units = [(layer, t) for layer in range(2) for t in range(count)]

    def part(ref, layer, start, size):
        return ref.at[layer, pl.ds(pl.multiple_of(start, 16), size)]

    def hop(u, stage):
        layer, t = units[u]
        rows = ins[t].shape[1]
        piece = rows // (8 if spread[t] else 4)
        base = core * (rows // 2)
        src = outs[t]
        if stage == 0:
            start = base + (zz * 2 + yy if spread[t] else yy) * piece
            size, dev, src = piece, to_x, ins[t]
        elif stage == 1:
            start = base + (zz * 2 + yy if spread[t] else yy) * piece
            size, dev = piece, to_y
        elif stage == 2:
            start, size, dev = base + zz * 2 * piece, 2 * piece, to_z
        else:
            start, size, dev = base, rows // 2, to_core
        return rdma(
            part(src, layer, start, size),
            part(outs[t], layer, start, size),
            sends.at[u, stage],
            recvs.at[u, stage],
            dev,
        )

    total = len(units)
    extra = rdma(small_in, small_out, sends.at[total, 0], recvs.at[total, 0], to_x)
    extra.start()
    for u in range(total):
        hop(u, 0).start()
    for step in range(total + 3):
        u = step - 2
        if 0 <= u < total:
            if spread[units[u][1]]:
                hop(u, 2).wait_recv()
            else:
                hop(u, 1).wait_recv()
            hop(u, 3).start()
        u = step - 1
        if 0 <= u < total and spread[units[u][1]]:
            hop(u, 1).wait_recv()
            hop(u, 2).start()
        u = step
        if u < total:
            hop(u, 0).wait_recv()
            hop(u, 1).start()
    extra.wait()
    for u in range(total):
        hop(u, 3).wait_recv()
        for stage in range(4):
            if stage != 2 or spread[units[u][1]]:
                hop(u, stage).wait_send()


def gather_weights(small, tensors, spread):
    count = len(tensors)
    any_spec = pl.BlockSpec(memory_space=pltpu.HBM)
    return pl.pallas_call(
        functools.partial(gather_kernel, spread),
        out_shape=[jax.ShapeDtypeStruct(a.shape, a.dtype) for a in (small, *tensors)],
        in_specs=[any_spec] * (1 + count),
        out_specs=[any_spec] * (1 + count),
        scratch_shapes=[
            pltpu.SemaphoreType.DMA((2 * count + 1, 4)),
            pltpu.SemaphoreType.DMA((2 * count + 1, 4)),
        ],
        compiler_params=pltpu.CompilerParams(collective_id=0, has_side_effects=True),
        name="gather_weights",
    )(small, *tensors)


def chunks_of(rows, dp):
    unit = 16 * dp
    units, out, at = rows // unit, [], 0
    while units > 0:
        size = 3 if units > 6 else (2 if units > 3 else 1)
        size = min(size, units)
        out.append((at, size * unit))
        at += size * unit
        units -= size
    return out


def reduce_kernel(dp, chunks, g, out, loc, cbuf, xbuf, ybuf, zbuf, cs, cr, xs, xr, ys, yr, zs, zr, bs, br, as_, ar, es, er, ls, os):
    Z = 4
    Y = dp // (2 * Z)
    d, x = lax.axis_index("dp"), lax.axis_index("mp")
    core, yy, zz = d % 2, (d // 2) % Y, d // (2 * Y)
    to_x = (d, 1 - x)
    to_core = (d + 1 - 2 * core, x)
    ys_peer = [(yy + i) % Y for i in range(1, Y)]
    zs_peer = [(zz + i) % Z for i in range(1, Z)]
    to_y = [((zz * Y + p) * 2 + core, x) for p in ys_peer]
    to_z = [((p * Y + yy) * 2 + core, x) for p in zs_peer]
    greet([to_core, to_x] + to_y + to_z)
    K = len(chunks)

    def al(v):
        return pl.multiple_of(v, 16)

    def sizes(k):
        at, rows = chunks[k]
        return at, rows, rows // 2, rows // 2 // Y, rows // 2 // Y // Z

    def core_copy(k):
        at, rows, half, _, _ = sizes(k)
        return rdma(
            g.at[:, pl.ds(al(at + (1 - core) * half), half)],
            cbuf.at[:, pl.ds(at // 2, half)],
            cs.at[k], cr.at[k], to_core,
        )

    def load(k):
        at, rows, half, _, _ = sizes(k)
        return pltpu.make_async_copy(
            g.at[:, pl.ds(al(at + core * half), half)], loc.at[k % 2, :, pl.ds(0, half)], ls.at[k % 2]
        )

    def x_copy(k):
        at, rows, half, _, _ = sizes(k)
        return rdma(cbuf.at[1, pl.ds(at // 2, half)], xbuf.at[pl.ds(at // 2, half)], xs.at[k], xr.at[k], to_x)

    def y_copy(k, i):
        at, rows, half, quarter, _ = sizes(k)
        base = at // (2 * Y) * (Y - 1)
        return rdma(
            cbuf.at[0, pl.ds(al(at // 2 + ys_peer[i] * quarter), quarter)],
            ybuf.at[pl.ds(base + i * quarter, quarter)],
            ys.at[k, i], yr.at[k, i], to_y[i],
        )

    def z_copy(k, i):
        at, rows, half, quarter, piece = sizes(k)
        base = at // (2 * Y * Z) * (Z - 1)
        return rdma(
            cbuf.at[0, pl.ds(al(at // 2 + yy * quarter + zs_peer[i] * piece), piece)],
            zbuf.at[pl.ds(base + i * piece, piece)],
            zs.at[k, i], zr.at[k, i], to_z[i],
        )

    def mine(k):
        at, rows, half, quarter, piece = sizes(k)
        return (
            pl.ds(al(at // 2 + yy * quarter + zz * piece), piece),
            pl.ds(al(at + core * half + yy * quarter + zz * piece), piece),
        )

    def own_copy(k):
        a, b = mine(k)
        return pltpu.make_async_copy(cbuf.at[0, a], out.at[b], os.at[k])

    def zb_copy(k, i):
        a, b = mine(k)
        return rdma(cbuf.at[0, a], out.at[b], bs.at[k, i], br.at[k, i], to_z[i])

    def yb_copy(k, i):
        at, rows, half, quarter, piece = sizes(k)
        rows_ = pl.ds(al(at + core * half + yy * quarter), quarter)
        return rdma(out.at[rows_], out.at[rows_], as_.at[k, i], ar.at[k, i], to_y[i])

    def cb_copy(k):
        at, rows, half, quarter, piece = sizes(k)
        rows_ = pl.ds(al(at + core * half), half)
        return rdma(out.at[rows_], out.at[rows_], es.at[k], er.at[k], to_core)

    f32, bf = jnp.float32, jnp.bfloat16

    def s1(k):
        at, rows, half, quarter, piece = sizes(k)
        if k + 1 < K:
            load(k + 1).start()
        load(k).wait()
        core_copy(k).wait_recv()
        for m in (1, 0):
            r = cbuf.at[m, pl.ds(at // 2, half)]
            r[...] = (r[...].astype(f32) + loc[k % 2, m, :half].astype(f32)).astype(bf)
            if m == 1:
                x_copy(k).start()

    def s2(k):
        at, rows, half, quarter, piece = sizes(k)
        x_copy(k).wait_recv()
        r = cbuf.at[0, pl.ds(at // 2, half)]
        r[...] = (r[...].astype(f32) + xbuf[at // 2 : at // 2 + half].astype(f32)).astype(bf)
        for i in range(Y - 1):
            y_copy(k, i).start()

    def s3(k):
        at, rows, half, quarter, piece = sizes(k)
        base = at // (2 * Y) * (Y - 1)
        r = cbuf.at[0, pl.ds(al(at // 2 + yy * quarter), quarter)]
        acc = r[...].astype(f32)
        for i in range(Y - 1):
            y_copy(k, i).wait_recv()
            acc = acc + ybuf[base + i * quarter : base + (i + 1) * quarter].astype(f32)
        r[...] = acc.astype(bf)
        for i in range(Z - 1):
            z_copy(k, i).start()

    def s4(k):
        at, rows, half, quarter, piece = sizes(k)
        base = at // (2 * Y * Z) * (Z - 1)
        a, b = mine(k)
        r = cbuf.at[0, a]
        acc = r[...].astype(f32)
        for i in range(Z - 1):
            z_copy(k, i).wait_recv()
            acc = acc + zbuf[base + i * piece : base + (i + 1) * piece].astype(f32)
        r[...] = acc.astype(bf)
        own_copy(k).start()
        for i in range(Z - 1):
            zb_copy(k, i).start()

    def s5(k):
        own_copy(k).wait()
        for i in range(Z - 1):
            zb_copy(k, i).wait_recv()
        for i in range(Y - 1):
            yb_copy(k, i).start()

    def s6(k):
        for i in range(Y - 1):
            yb_copy(k, i).wait_recv()
        cb_copy(k).start()

    for k in range(K):
        core_copy(k).start()
    load(0).start()
    stages = [s1, s2, s3, s4, s5, s6]
    lag = [0, 4, 5, 6, 7, 8]
    for t in range(K + lag[-1]):
        for stage, off in reversed(list(zip(stages, lag))):
            if 0 <= t - off < K:
                stage(t - off)
    for k in range(K):
        cb_copy(k).wait_recv()
        core_copy(k).wait_send()
        x_copy(k).wait_send()
        cb_copy(k).wait_send()
        for i in range(Y - 1):
            y_copy(k, i).wait_send()
            yb_copy(k, i).wait_send()
        for i in range(Z - 1):
            z_copy(k, i).wait_send()
            zb_copy(k, i).wait_send()


def reduce_gradients(dp, packed):
    rows = packed.shape[1]
    chunks = chunks_of(rows, dp)
    K = len(chunks)
    Z = 4
    Y = dp // (2 * Z)
    biggest = max(size for _, size in chunks) // 2
    hbm = pl.BlockSpec(memory_space=pltpu.HBM)
    bf = jnp.bfloat16
    dma = pltpu.SemaphoreType.DMA
    return pl.pallas_call(
        functools.partial(reduce_kernel, dp, chunks),
        out_shape=jax.ShapeDtypeStruct((rows, W), bf),
        in_specs=[hbm],
        out_specs=hbm,
        scratch_shapes=[
            pltpu.VMEM((2, 2, biggest, W), bf),
            pltpu.VMEM((2, rows // 2, W), bf),
            pltpu.VMEM((rows // 2, W), bf),
            pltpu.VMEM((rows // (2 * Y) * (Y - 1), W), bf),
            pltpu.VMEM((rows // (2 * Y * Z) * (Z - 1), W), bf),
            dma((K,)), dma((K,)), dma((K,)), dma((K,)),
            dma((K, Y - 1)), dma((K, Y - 1)),
            dma((K, Z - 1)), dma((K, Z - 1)),
            dma((K, Z - 1)), dma((K, Z - 1)),
            dma((K, Y - 1)), dma((K, Y - 1)),
            dma((K,)), dma((K,)), dma((2,)), dma((K,)),
        ],
        compiler_params=pltpu.CompilerParams(
            collective_id=1, has_side_effects=True, vmem_limit_bytes=56 * 2**20
        ),
        name="reduce_gradients",
    )(packed)


def layer_norm(values, scaling, shifting):
    average = jnp.mean(values, axis=-1, keepdims=True)
    centred = values - average
    spread = jnp.mean(centred * centred, axis=-1, keepdims=True)
    return centred * lax.rsqrt(spread + 1e-05) * scaling + shifting


def positions(lengths_row, row_count, head_size):
    finish = jnp.cumsum(lengths_row, dtype=jnp.int32)
    counter = jnp.arange(row_count, dtype=jnp.int32)
    passed = counter[:, None] >= finish[None, :]
    segment = jnp.sum(passed.astype(jnp.int32), axis=1, dtype=jnp.int32)
    start_at = jnp.sum(jnp.where(passed, lengths_row[None, :], 0), axis=1, dtype=jnp.int32)
    offset = (counter - start_at).astype(jnp.float32)
    half_size = head_size // 2
    frequency = jnp.exp(
        jnp.arange(half_size, dtype=jnp.float32) * (-2.0 * math.log(10000.0) / head_size)
    )
    angles = offset[:, None] * frequency[None, :]
    same_mol = (segment[:, None] == segment[None, :]).astype(jnp.float32)
    return (jnp.cos(angles)[:, None, :], jnp.sin(angles)[:, None, :], same_mol)


def rotate(vectors, cosines, sines):
    half_size = vectors.shape[-1] // 2
    leading = vectors[..., :half_size]
    trailing = vectors[..., half_size:]
    return jnp.concatenate(
        [leading * cosines - trailing * sines, trailing * cosines + leading * sines], axis=-1
    )


def features(vectors, random_proj):
    scaled = vectors * vectors.shape[-1] ** (-0.25)
    return jax.nn.softplus(
        jnp.einsum("thd,hdm->thm", scaled, random_proj, precision=lax.Precision.HIGH)
    )


def attend(queries, key_rows, values, random_proj, cosines, sines, same_mol):
    row_count, model_width = queries.shape
    head_count, head_size = (random_proj.shape[0], random_proj.shape[1])
    shaped = (row_count, head_count, head_size)
    query_feats = features(rotate(queries.reshape(shaped), cosines, sines), random_proj)
    key_feats = features(rotate(key_rows.reshape(shaped), cosines, sines), random_proj)
    scores = jnp.einsum("thm,shm->hts", query_feats, key_feats) * same_mol[None]
    numerator = jnp.einsum("hts,shd->thd", scores, values.reshape(shaped))
    denominator = jnp.sum(scores, axis=2).T[:, :, None]
    return (numerator / denominator).reshape(row_count, model_width)


def gelu_exact(values):
    return jax.nn.gelu(values, approximate=False)


def on_device(
    dp,
    tokens,
    cotangent,
    lengths,
    random_proj,
    attn_weight,
    attn_bias,
    out_weight,
    norm_gains,
    biases,
    up_weight,
    up_bias,
    down_weight,
):
    f32, bf = jnp.float32, jnp.bfloat16
    layers = attn_weight.shape[0]
    model = tokens.shape[1]
    part = attn_weight.shape[3]
    hidden_part = up_weight.shape[2]
    blocks = hidden_part // part
    x = lax.axis_index("mp")
    heads = random_proj.shape[1] // 2
    small = jnp.concatenate(
        [
            attn_bias.reshape(-1, part),
            up_bias.reshape(-1, part),
            jnp.zeros((16 - layers * (3 + blocks), part), bf),
        ]
    )
    gathered = gather_weights(
        small,
        (attn_weight.reshape(layers, -1, part), out_weight, up_weight, down_weight),
        (True, True, False, True),
    )
    other_attn_bias = gathered[0][: 3 * layers].reshape(layers, 3, part)
    other_up_bias = gathered[0][3 * layers : (3 + blocks) * layers].reshape(layers, hidden_part)
    other_attn = gathered[1].reshape(attn_weight.shape)
    attn_b = jnp.concatenate([attn_bias, other_attn_bias], axis=2).astype(f32)
    up_b = jnp.concatenate([up_bias, other_up_bias], axis=1).astype(f32)
    attn_w = jnp.concatenate([attn_weight, other_attn], axis=3)
    out_w = jnp.concatenate([out_weight, gathered[2]], axis=1)
    up_w = jnp.concatenate([up_weight, gathered[3]], axis=2)
    down_w = jnp.concatenate([down_weight, gathered[4]], axis=1)
    proj = jnp.where(x == 0, random_proj, jnp.roll(random_proj, heads, axis=1))
    gain_values = norm_gains.astype(f32)
    shift_values = biases.astype(f32)
    cosines, sines, same_mol = positions(lengths[0], tokens.shape[0], random_proj.shape[2])
    current = tokens.astype(f32)
    kept = []
    for layer in range(layers):
        normed = layer_norm(current, gain_values[layer, 0], shift_values[layer, 0]).astype(bf)
        projected = [
            jnp.dot(normed, attn_w[layer, j], preferred_element_type=f32) + attn_b[layer, j]
            for j in range(3)
        ]
        context = attend(*projected, proj[layer], cosines, sines, same_mol).astype(bf)
        middle = (
            current
            + jnp.dot(context, out_w[layer], preferred_element_type=f32)
            + shift_values[layer, 1]
        )
        second = layer_norm(middle, gain_values[layer, 1], shift_values[layer, 2]).astype(bf)
        hidden = jnp.dot(second, up_w[layer], preferred_element_type=f32) + up_b[layer]
        active = gelu_exact(hidden).astype(bf)
        kept.append((current, normed, projected, context, middle, second, hidden, active))
        current = (
            middle
            + jnp.dot(active, down_w[layer], preferred_element_type=f32)
            + shift_values[layer, 3]
        )
    stack_out = current.astype(bf)
    grad_now = cotangent.astype(f32)
    rows = []
    smalls = []

    def halves(grad, axis):
        return jnp.split(grad.astype(bf), 2, axis=axis)

    for layer in reversed(range(layers)):
        layer_in, normed, projected, context, middle, second, hidden, active = kept[layer]
        branch_grad = grad_now.astype(bf)
        down_grad = jnp.dot(active.T, branch_grad, preferred_element_type=f32).astype(bf)
        active_grad = jnp.dot(branch_grad, down_w[layer].T, preferred_element_type=f32)
        hidden_grad = jax.vjp(gelu_exact, hidden)[1](active_grad)[0].astype(bf)
        up_grad = jnp.dot(second.T, hidden_grad, preferred_element_type=f32).astype(bf)
        up_shift_grad = jnp.sum(hidden_grad.astype(f32), axis=0)
        second_grad = jnp.dot(hidden_grad, up_w[layer].T, preferred_element_type=f32)
        middle_grad, gain_two, shift_two = jax.vjp(
            layer_norm, middle, gain_values[layer, 1], shift_values[layer, 2]
        )[1](second_grad)
        middle_grad = middle_grad + grad_now
        attn_grad = middle_grad.astype(bf)
        out_grad = jnp.dot(context.T, attn_grad, preferred_element_type=f32).astype(bf)
        context_grad = jnp.dot(attn_grad, out_w[layer].T, preferred_element_type=f32)

        def attend_local(queries, key_rows, values):
            return attend(queries, key_rows, values, proj[layer], cosines, sines, same_mol)

        triple = [g.astype(bf) for g in jax.vjp(attend_local, *projected)[1](context_grad)]
        attn_grads = [
            jnp.dot(normed.T, g, preferred_element_type=f32).astype(bf) for g in triple
        ]
        attn_bias_grad = jnp.stack([jnp.sum(g.astype(f32), axis=0) for g in triple])
        normed_grad = sum(
            jnp.dot(triple[j], attn_w[layer, j].T, preferred_element_type=f32) for j in range(3)
        )
        input_grad, gain_one, shift_one = jax.vjp(
            layer_norm, layer_in, gain_values[layer, 0], shift_values[layer, 0]
        )[1](normed_grad)
        full_rows = jnp.stack(
            [
                gain_one,
                gain_two,
                shift_one,
                jnp.sum(attn_grad.astype(f32), axis=0),
                shift_two,
                jnp.sum(branch_grad.astype(f32), axis=0),
            ]
        ).reshape(6, 2, part)
        full_rows = jnp.where(x == 0, full_rows, full_rows[:, ::-1])
        small_rows = jnp.concatenate(
            [
                full_rows,
                attn_bias_grad.reshape(3, 2, part),
                up_shift_grad.reshape(2, blocks, part).swapaxes(0, 1),
            ]
        ).swapaxes(0, 1)
        smalls.append(small_rows.astype(bf))
        grad_now = input_grad + middle_grad
        rows.append(
            [
                jnp.stack(
                    [jnp.concatenate([a[:, i * part : (i + 1) * part] for i in range(2)]) for a in halves(down_grad, 0)]
                ),
                jnp.stack(
                    [jnp.concatenate([a[:, i * part : (i + 1) * part] for i in range(blocks)]) for a in halves(up_grad, 1)]
                ),
                jnp.stack(
                    [jnp.concatenate([a[:, i * part : (i + 1) * part] for i in range(2)]) for a in halves(out_grad, 0)]
                ),
                jnp.stack(
                    [jnp.concatenate([a[:, i * part : (i + 1) * part] for a in attn_grads]) for i in range(2)]
                ),
            ]
        )
    small_rows = jnp.concatenate(smalls, axis=1)
    pad = 16 * dp - small_rows.shape[1]
    small_rows = jnp.pad(small_rows, ((0, 0), (0, pad), (0, 0)))
    packed = jnp.concatenate(rows[0] + rows[1] + [small_rows], axis=1)
    reduced = reduce_gradients(dp, packed)
    at = 0

    def take(count):
        nonlocal at
        block = reduced[at : at + count]
        at += count
        return block

    def columns(block, count):
        return jnp.concatenate(jnp.split(block, count), axis=1).astype(f32)

    found = [None] * layers
    for layer in reversed(range(layers)):
        down_g = columns(take(2 * hidden_part), 2)
        up_g = columns(take(blocks * model), blocks)
        out_g = columns(take(2 * part), 2)
        attn_g = take(3 * model).reshape(3, model, part).astype(f32)
        found[layer] = [attn_g, out_g, up_g, down_g]
    small_g = []
    for _ in range(layers):
        small_g.append(take(9 + blocks).astype(f32))
    small_g = jnp.stack(small_g[::-1])
    big = [jnp.stack([found[layer][i] for layer in range(layers)]) for i in range(4)]
    return (
        stack_out,
        grad_now,
        big[0],
        small_g[:, 6:9],
        big[1],
        small_g[:, :2],
        small_g[:, 2:6],
        big[2],
        small_g[:, 9 : 9 + blocks].reshape(layers, hidden_part),
        big[3],
    )


def solution(mesh):
    return jax.shard_map(
        functools.partial(on_device, mesh.shape["dp"]),
        mesh=mesh,
        in_specs=(
            P(("dp", "mp"), None),
            P(("dp", "mp"), None),
            P(("dp", "mp"), None),
            P(),
            P(None, None, None, "mp"),
            P(None, None, "mp"),
            P(None, "mp", None),
            P(),
            P(),
            P(None, None, "mp"),
            P(None, "mp"),
            P(None, "mp", None),
        ),
        out_specs=(
            P(("dp", "mp"), None),
            P(("dp", "mp"), None),
            P(None, None, None, "mp"),
            P(None, None, "mp"),
            P(None, "mp", None),
            P(None, None, "mp"),
            P(None, None, "mp"),
            P(None, None, "mp"),
            P(None, "mp"),
            P(None, "mp", None),
        ),
        check_vma=False,
    )
```

```python
import functools
import math

import jax
import jax.numpy as jnp
from jax import lax
from jax.experimental import pallas as pl
from jax.experimental.pallas import tpu as pltpu
from jax.sharding import PartitionSpec as P

MESH = pl.DeviceIdType.MESH
f32, bf = jnp.float32, jnp.bfloat16
TOK, D, HEADS, HD, FEATS = 256, 768, 12, 64, 32
W = D // 2
FF = 4 * D
RING = 4 * D
LAYER_ROWS = 12 * D
LAG = 2
STAGES = [1, 3, 5, 7, 9, 11]
CUTS = (1, 1, 2, 2)
Z = 4


def rdma(src, dst, send, recv, dev):
    return pltpu.make_async_remote_copy(
        src_ref=src, dst_ref=dst, send_sem=send, recv_sem=recv, device_id=dev, device_id_type=MESH
    )


def dot_nn(a, b):
    return jnp.dot(a, b, preferred_element_type=f32)


def dot_nt(a, b):
    return lax.dot_general(a, b, (((1,), (1,)), ((), ())), preferred_element_type=f32)


def dot_tn(a, b):
    return lax.dot_general(a, b, (((0,), (0,)), ((), ())), preferred_element_type=f32)


def split_two(v):
    high = v.astype(bf)
    return high, (v - high.astype(f32)).astype(bf)


def al(v, m=16):
    return pl.multiple_of(v, m)


def chunks_of(dp):
    step = 3 * D if dp < 16 else (16 * dp if dp > 16 else D)
    out = [(at, step) for at in range(0, 2 * LAYER_ROWS, step)]
    return out + [(2 * LAYER_ROWS, 16 * dp)]


def gather_groups(rows):
    groups = []
    for layer in range(2):
        for t in range(4):
            size = rows[t] // CUTS[t]
            for cut in range(CUTS[t]):
                third = size // 3
                groups.append(
                    [(layer, t, cut * size, third, False), (layer, t, cut * size + third, size - third, True)]
                )
    return groups


def rows_loop(body, tile, init=0):
    def step(i, carry):
        return body(pl.ds(al(i * tile, tile), tile), carry)

    return lax.fori_loop(0, TOK // tile, step, init)


def fold(v):
    return jnp.sum(v.reshape(v.shape[0] // 8, 8, v.shape[1]), axis=0)


def main_kernel(
    dp, chunks,
    lengths, tokens, cotangent, proj, own_small, gains, shifts,
    own_a, own_o, own_u, own_d,
    stack_out, tokens_grad, reduced, oth_a, oth_o, oth_u, oth_d, cland, xland,
    oth_small, wq, wo, wu, wd,
    X, mid, nrm, sec, qf, kf, sq, sk, vv, rden, ctx, act, dgl,
    pbh, pbl, mask, cosv, sinv, t0, t1, t2, gn, gq, trans, sm,
    stage, acc, xsend, cslot, xslot, ybuf, zbuf,
    gs, gr, wsem, cs, cr, cl, xs, xr, xl, ys, yr, zs, zr, bs, br, as_, ar, es, er, os,
):
    Y = dp // (2 * Z)
    d, x = lax.axis_index("dp"), lax.axis_index("mp")
    core = d % 2
    yy, zz = (d // 2) % Y, d // (2 * Y)
    ys_peer = [(yy + i) % Y for i in range(1, Y)]
    zs_peer = [(zz + i) % Z for i in range(1, Z)]
    to_x = (d, 1 - x)
    to_core = (d + 1 - 2 * core, x)
    to_y = [((zz * Y + p) * 2 + core, x) for p in ys_peer]
    to_z = [((p * Y + yy) * 2 + core, x) for p in zs_peer]
    peers = [to_core, to_x] + to_y + to_z
    barrier = pltpu.get_barrier_semaphore()
    for peer in peers:
        pl.semaphore_signal(barrier, inc=1, device_id=peer, device_id_type=MESH)
    pl.semaphore_wait(barrier, len(peers))

    own = (own_a, own_o, own_u, own_d)
    oth = (oth_a, oth_o, oth_u, oth_d)
    y1, z1 = (d // 2) % 2, (d // 4) % 2
    gather_y = (d + 2 - 4 * y1, x)
    gather_z = (d + 4 - 8 * z1, x)
    groups = gather_groups([r.shape[1] for r in own])
    G = len(groups)

    def hop(u, i, stage_):
        layer, t, first, rows, wide = groups[u][i]
        piece = rows // (8 if wide else 4)
        base = first + core * (rows // 2)
        src = oth[t]
        if stage_ == 0:
            start = base + (z1 * 2 + y1 if wide else y1) * piece
            size, dev, src = piece, to_x, own[t]
        elif stage_ == 1:
            start = base + (z1 * 2 + y1 if wide else y1) * piece
            size, dev = piece, gather_y
        elif stage_ == 2:
            start, size, dev = base + z1 * 2 * piece, 2 * piece, gather_z
        else:
            start, size, dev = base, rows // 2, to_core
        return rdma(
            src.at[layer, pl.ds(al(start), size)],
            oth[t].at[layer, pl.ds(al(start), size)],
            gs.at[u, 4 * i + stage_],
            gr.at[u, 4 * i + stage_],
            dev,
        )

    small_copy = rdma(own_small, oth_small, gs.at[G, 0], gr.at[G, 0], to_x)
    small_copy.start()
    for u in range(G):
        hop(u, 0, 0).start()
        hop(u, 1, 0).start()
    pumped = [0]

    def pump(count):
        for step in range(pumped[0], min(pumped[0] + count, G + 2 * LAG)):
            u = step - 2 * LAG
            if 0 <= u < G:
                hop(u, 1, 2).wait_recv()
                hop(u, 1, 3).start()
            u = step - LAG
            if 0 <= u < G:
                hop(u, 1, 1).wait_recv()
                hop(u, 1, 2).start()
                hop(u, 0, 1).wait_recv()
                hop(u, 0, 3).start()
            u = step
            if u < G:
                hop(u, 1, 0).wait_recv()
                hop(u, 1, 1).start()
                hop(u, 0, 0).wait_recv()
                hop(u, 0, 1).start()
            pumped[0] = step + 1

    def weight_copies(t, layer, mine):
        src = (own if mine else oth)[t].at[layer]
        m = 0 if mine else 1
        sem = wsem.at[t, m]
        if t == 0:
            return [
                pltpu.make_async_copy(
                    src.at[pl.ds(j * D, D)], wq.at[j, :, pl.ds(m * W, W)], wsem.at[4 + j, m]
                )
                for j in range(3)
            ]
        if t == 1:
            return [pltpu.make_async_copy(src, wo.at[pl.ds(m * W, W)], sem)]
        if t == 2:
            return [pltpu.make_async_copy(src, wu.at[:, pl.ds(m * (FF // 2), FF // 2)], sem)]
        return [pltpu.make_async_copy(src, wd.at[pl.ds(m * (FF // 2), FF // 2)], sem)]

    def load_weight(t, layer, mine):
        for c in weight_copies(t, layer, mine):
            c.start()

    def wait_weight(t, layer):
        for mine in (True, False):
            for c in weight_copies(t, layer, mine):
                c.wait()

    def arrived(t, layer):
        for u in range(G):
            if groups[u][0][:2] == (layer, t):
                hop(u, 0, 3).wait_recv()
                hop(u, 1, 3).wait_recv()
        load_weight(t, layer, False)

    K = len(chunks)
    slot_rows = max(size for _, size in chunks) // 2

    def sizes(k):
        at, rows = chunks[k]
        return at, rows, rows // 2, rows // 2 // Y, rows // 2 // Y // Z

    def core_copy(k):
        at, rows, half, _, _ = sizes(k)
        return rdma(
            stage.at[:, pl.ds(al(at % RING + (1 - core) * half), half)],
            cland.at[:, pl.ds(at // 2, half)],
            cs.at[k], cr.at[k], to_core,
        )

    def core_load(k):
        at, rows, half, _, _ = sizes(k)
        return pltpu.make_async_copy(
            cland.at[:, pl.ds(at // 2, half)], cslot.at[:, pl.ds(0, half)], cl.at[0]
        )

    def x_copy(k):
        at, rows, half, _, _ = sizes(k)
        return rdma(
            xsend.at[k % 4, pl.ds(0, half)], xland.at[pl.ds(at // 2, half)], xs.at[k], xr.at[k], to_x
        )

    def x_load(k):
        at, rows, half, _, _ = sizes(k)
        return pltpu.make_async_copy(
            xland.at[pl.ds(at // 2, half)], xslot.at[pl.ds(0, half)], xl.at[0]
        )

    def y_copy(k, i):
        at, rows, half, quarter, _ = sizes(k)
        base = at // (2 * Y) * (Y - 1)
        return rdma(
            acc.at[pl.ds(al(at // 2 + ys_peer[i] * quarter), quarter)],
            ybuf.at[pl.ds(base + i * quarter, quarter)],
            ys.at[k, i], yr.at[k, i], to_y[i],
        )

    def z_copy(k, i):
        at, rows, half, quarter, piece = sizes(k)
        base = at // (2 * Y * Z) * (Z - 1)
        return rdma(
            acc.at[pl.ds(al(at // 2 + yy * quarter + zs_peer[i] * piece), piece)],
            zbuf.at[pl.ds(base + i * piece, piece)],
            zs.at[k, i], zr.at[k, i], to_z[i],
        )

    def mine_rows(k):
        at, rows, half, quarter, piece = sizes(k)
        return (
            pl.ds(al(at // 2 + yy * quarter + zz * piece), piece),
            pl.ds(al(at + core * half + yy * quarter + zz * piece), piece),
        )

    def own_copy(k):
        a, b = mine_rows(k)
        return pltpu.make_async_copy(acc.at[a], reduced.at[b], os.at[k])

    def zb_copy(k, i):
        a, b = mine_rows(k)
        return rdma(acc.at[a], reduced.at[b], bs.at[k, i], br.at[k, i], to_z[i])

    def yb_copy(k, i):
        at, rows, half, quarter, piece = sizes(k)
        r = pl.ds(al(at + core * half + yy * quarter), quarter)
        return rdma(reduced.at[r], reduced.at[r], as_.at[k, i], ar.at[k, i], to_y[i])

    def cb_copy(k):
        at, rows, half, quarter, piece = sizes(k)
        r = pl.ds(al(at + core * half), half)
        return rdma(reduced.at[r], reduced.at[r], es.at[k], er.at[k], to_core)

    def add_rows(total, dst, dst_at, srcs):
        tile = 16
        for size in (128, 96, 64, 48, 32):
            if total % size == 0:
                tile = size
                break

        def body(i, carry):
            r0 = i * tile
            v = None
            for ref, at in srcs:
                part = ref[pl.ds(al(at + r0), tile)].astype(f32)
                v = part if v is None else v + part
            dst[pl.ds(al(dst_at + r0), tile)] = v.astype(bf)
            return carry

        lax.fori_loop(0, total // tile, body, 0)

    def s1(k):
        at, rows, half, quarter, piece = sizes(k)
        core_copy(k).wait_recv()
        core_load(k).start()
        if k >= 4:
            x_copy(k - 4).wait_send()
        core_load(k).wait()
        here = at % RING + core * half
        add_rows(half, xsend.at[k % 4], 0, [(stage.at[1], here), (cslot.at[1], 0)])
        x_copy(k).start()
        add_rows(half, acc, at // 2, [(stage.at[0], here), (cslot.at[0], 0)])

    def s2(k):
        at, rows, half, quarter, piece = sizes(k)
        x_copy(k).wait_recv()
        x_load(k).start()
        x_load(k).wait()
        add_rows(half, acc, at // 2, [(acc, at // 2), (xslot, 0)])
        for i in range(Y - 1):
            y_copy(k, i).start()

    def s3(k):
        at, rows, half, quarter, piece = sizes(k)
        base = at // (2 * Y) * (Y - 1)
        for i in range(Y - 1):
            y_copy(k, i).wait_recv()
        here = at // 2 + yy * quarter
        add_rows(quarter, acc, here, [(acc, here)] + [(ybuf, base + i * quarter) for i in range(Y - 1)])
        for i in range(Z - 1):
            z_copy(k, i).start()

    def s4(k):
        at, rows, half, quarter, piece = sizes(k)
        base = at // (2 * Y * Z) * (Z - 1)
        for i in range(Z - 1):
            z_copy(k, i).wait_recv()
        here = at // 2 + yy * quarter + zz * piece
        add_rows(piece, acc, here, [(acc, here)] + [(zbuf, base + i * piece) for i in range(Z - 1)])
        own_copy(k).start()
        for i in range(Z - 1):
            zb_copy(k, i).start()

    def s5(k):
        own_copy(k).wait()
        for i in range(Z - 1):
            zb_copy(k, i).wait_recv()
        for i in range(Y - 1):
            yb_copy(k, i).start()

    def s6(k):
        for i in range(Y - 1):
            yb_copy(k, i).wait_recv()
        cb_copy(k).start()

    ticked = [0]
    settled = [0]

    def settle(k):
        while settled[0] <= k:
            s1(settled[0])
            core_copy(settled[0]).wait_send()
            settled[0] += 1

    def tick():
        t = ticked[0]
        ticked[0] += 1
        for fn, off in reversed(list(zip([s2, s3, s4, s5, s6], STAGES[1:]))):
            if 0 <= t - off < K:
                fn(t - off)
        if 0 <= t - STAGES[0] < K:
            settle(t - STAGES[0])

    made = [0]

    def reserve(start, size):
        assert all(settled[0] > k for k in range(K) if chunks[k][0] < start + size - RING)

    def produced(upto):
        made[0] = upto
        while ticked[0] < K and chunks[ticked[0]][0] + chunks[ticked[0]][1] <= upto:
            core_copy(ticked[0]).start()
            tick()

    for t in range(4):
        load_weight(t, 0, True)
    row_i = lax.broadcasted_iota(jnp.int32, (TOK, 128), 0)
    lane = lax.broadcasted_iota(jnp.int32, (TOK, 128), 1)
    lane_row = lax.broadcasted_iota(jnp.int32, (1, 128), 1)
    seg_r = jnp.zeros((TOK, 1), jnp.int32)
    seg_c = jnp.zeros((1, TOK), jnp.int32)
    begin = jnp.zeros((TOK, 128), jnp.int32)
    r1 = lax.broadcasted_iota(jnp.int32, (TOK, 1), 0)
    c1 = lax.broadcasted_iota(jnp.int32, (1, TOK), 1)
    finish = jnp.int32(0)
    for i in range(8):
        size = lengths[0, i]
        finish = finish + size
        seg_r = seg_r + jnp.where(r1 >= finish, 1, 0)
        seg_c = seg_c + jnp.where(c1 >= finish, 1, 0)
        begin = begin + jnp.where(row_i >= finish, size, 0)
    mask[...] = jnp.where(seg_r == seg_c, 1.0, 0.0).astype(f32)
    place = (row_i - begin).astype(f32)
    freq = jnp.exp((lane % (HD // 2)).astype(f32) * (-2.0 * math.log(10000.0) / HD))
    angle = place * freq
    low_half = (lane % HD) < (HD // 2)
    cosv[...] = jnp.cos(angle)
    sn = jnp.sin(angle)
    sinv[...] = jnp.where(low_half, -sn, sn)
    low_row = (lane_row % HD) < (HD // 2)
    four = [jnp.where(lane_row // FEATS == i, 1.0, 0.0).astype(bf) for i in range(4)]
    two = [jnp.where(lane_row // HD == i, 1.0, 0.0).astype(f32) for i in range(2)]

    block_row = lax.broadcasted_iota(jnp.int32, (256, 128), 0) // HD
    block_col = lax.broadcasted_iota(jnp.int32, (256, 128), 1) // FEATS
    diag = jnp.where(block_row == block_col, HD ** -0.25, 0.0).astype(f32)
    for layer in range(2):
        for g in range(3):
            pieces = []
            for i in range(4):
                h = 4 * g + i
                half_at = x * W if h < 6 else (1 - x) * W
                at = half_at + (h % 6) * HD
                pieces.append(proj[layer, pl.ds(al(at, 8), HD), :])
            p = jnp.concatenate(pieces, axis=0)
            p = jnp.concatenate([p] * 4, axis=1) * diag
            hi, lo = split_two(p)
            pbh[layer, g] = hi
            pbl[layer, g] = lo

    def swap(u):
        return jnp.where(low_row, pltpu.roll(u, 96, 1), pltpu.roll(u, 32, 1))

    def col128(at):
        return pl.ds(at, 128)

    def bias_row(row):
        return jnp.concatenate([own_small[row : row + 1, :], oth_small[row : row + 1, :]], axis=1)

    def up_bias_row(layer, m, i):
        src = own_small if m == 0 else oth_small
        r = 6 + 4 * layer + 2 * i
        return jnp.concatenate([src[r : r + 1, :], src[r + 1 : r + 2, :]], axis=1)

    def gain(layer, i):
        return gains[2 * layer + i : 2 * layer + i + 1, :]

    def shift(layer, i):
        return shifts[4 * layer + i : 4 * layer + i + 1, :]

    def norm_into(src, layer, i, dst):
        g, b = gain(layer, i), shift(layer, 2 * i)

        def body(rows, carry):
            v = src[layer, rows, :]
            c = v - jnp.mean(v, axis=-1, keepdims=True)
            r = lax.rsqrt(jnp.mean(c * c, axis=-1, keepdims=True) + 1e-05)
            dst[layer, rows, :] = (c * r * g + b).astype(bf)
            return carry

        rows_loop(body, 32)

    def project(layer):
        norm_into(X, layer, 0, nrm)
        t0[...] = dot_nn(nrm[layer], wq[0]) + bias_row(3 * layer)
        t1[...] = dot_nn(nrm[layer], wq[1]) + bias_row(3 * layer + 1)
        vv[layer] = (dot_nn(nrm[layer], wq[2]) + bias_row(3 * layer + 2)).astype(bf)

    def feature(src, layer, g, feat, sig):
        parts = []
        for p in range(2):
            u = src[:, col128(256 * g + 128 * p)]
            parts.append(u * cosv[...] + swap(u) * sinv[...])
        hi, lo = split_two(jnp.concatenate(parts, axis=1))
        z = dot_nn(hi, pbh[layer, g]) + dot_nn(lo, pbh[layer, g]) + dot_nn(hi, pbl[layer, g])
        f = jnp.maximum(z, 0.0) + jnp.log1p(jnp.exp(-jnp.abs(z)))
        feat[layer, :, col128(128 * g)] = f.astype(bf)
        sig[layer, :, col128(128 * g)] = jnp.exp(z - f)

    def scores(layer, g, i):
        q = qf[layer, :, col128(128 * g)] * four[i]
        return (dot_nt(q, kf[layer, :, col128(128 * g)]) * mask[...]).astype(bf)

    def attention(layer, g):
        feature(t0, layer, g, qf, sq)
        feature(t1, layer, g, kf, sk)
        ones = jnp.ones((TOK, 128), bf)
        for p in range(2):
            cols = col128(256 * g + 128 * p)
            right = jnp.concatenate([vv[layer, :, cols], ones], axis=1)
            a = dot_nn(scores(layer, g, 2 * p), right)
            b = dot_nn(scores(layer, g, 2 * p + 1), right)
            first = lane_row < HD
            num = jnp.where(first, a[:, :128], b[:, :128])
            den = jnp.where(first, a[:, 128:], b[:, 128:])
            r = 1.0 / den
            rden[layer, :, cols] = r
            ctx[layer, :, cols] = num * r

    def out_project(layer):
        mid[layer] = X[layer] + dot_nn(ctx[layer].astype(bf), wo[...]) + shift(layer, 1)
        norm_into(mid, layer, 1, sec)

    def feed(layer, m, i):
        cols = pl.ds(m * (FF // 2) + i * D, D)
        t0[...] = dot_nn(sec[layer], wu[:, cols])
        b = up_bias_row(layer, m, i)

        def body(rows, carry):
            h = t0[rows, :] + b
            phi = 0.5 + 0.5 * lax.erf(h * (2.0 ** -0.5))
            act[layer, rows, cols] = (h * phi).astype(bf)
            dgl[layer, rows, cols] = (
                phi + h * (jnp.exp(-0.5 * h * h) * ((2.0 * math.pi) ** -0.5))
            ).astype(bf)
            return carry

        rows_loop(body, 16)
        part = dot_nn(act[layer, :, cols], wd[cols, :])
        if (m, i) == (0, 0):
            t2[...] = part + mid[layer] + shift(layer, 3)
        else:
            t2[...] += part

    X[0] = tokens[...].astype(f32)
    pump(6)
    arrived(0, 0)
    small_copy.wait()
    wait_weight(0, 0)
    for layer in range(2):
        if layer:
            wait_weight(0, 1)
        project(layer)
        if layer == 0:
            load_weight(0, 1, True)
        pump(1)
        attention(layer, 0)
        pump(1)
        attention(layer, 1)
        attention(layer, 2)
        if layer == 0:
            arrived(1, 0)
        pump(1)
        wait_weight(1, layer)
        out_project(layer)
        if layer == 0:
            load_weight(1, 1, True)
        pump(2 if layer == 0 else 16)
        if layer == 0:
            arrived(2, 0)
            arrived(3, 0)
        else:
            arrived(2, 1)
            arrived(3, 1)
        wait_weight(2, layer)
        wait_weight(3, layer)
        for m in range(2):
            for i in range(2):
                feed(layer, m, i)
            pump(1 if layer == 0 else 0)
        if layer == 0:
            load_weight(2, 1, True)
            load_weight(3, 1, True)
            X[1] = t2[...]
            arrived(0, 1)
            arrived(1, 1)
        else:
            stack_out[...] = t2[...].astype(bf)

    sm[...] = jnp.zeros_like(sm)

    def full_row(row, v):
        first, second = v[:, :W], v[:, W:]
        sm[0, row : row + 1, :] = jnp.where(x == 0, first, second)
        sm[1, row : row + 1, :] = jnp.where(x == 0, second, first)

    def norm_back(layer, i, src, up, base, dst, base_row):
        g = gain(layer, i)
        zero = jnp.zeros((8, D), f32)

        def body(rows, carry):
            v = src[layer, rows, :]
            u = up[rows, :]
            c = v - jnp.mean(v, axis=-1, keepdims=True)
            r = lax.rsqrt(jnp.mean(c * c, axis=-1, keepdims=True) + 1e-05)
            hat = c * r
            dh = u * g
            dv = r * (
                dh
                - jnp.mean(dh, axis=-1, keepdims=True)
                - hat * jnp.mean(dh * hat, axis=-1, keepdims=True)
            )
            dst[rows, :] = base[rows, :] + dv
            return (carry[0] + fold(u * hat), carry[1] + fold(u))

        a, b = rows_loop(body, 32, (zero, zero))
        full_row(base_row + i, jnp.sum(a, axis=0, keepdims=True))
        full_row(base_row + 2 + 2 * i, jnp.sum(b, axis=0, keepdims=True))

    def column_sum(v):
        return jnp.sum(v.astype(f32), axis=0, keepdims=True)

    def put(m, row, v):
        stage[m, pl.ds(row % RING, v.shape[0]), :] = v.astype(bf)

    gn[...] = cotangent[...].astype(f32)
    for layer in (1, 0):
        row0 = (1 - layer) * LAYER_ROWS
        small_row = (1 - layer) * 13
        if layer == 0:
            wait_weight(3, 0)
            wait_weight(2, 0)
        fg = gq.at[0]
        fg[...] = gn[...].astype(bf)
        full_row(small_row + 5, column_sum(gn[...].astype(bf)))
        st = trans.at[1]
        st[...] = sec[layer].T
        for i in range(2):
            at = row0 + i * RING
            reserve(at, 2 * D)
            for m in range(2):
                cols = pl.ds(m * (FF // 2) + i * D, D)
                trans[0] = act[layer, :, cols].T
                for half in range(2):
                    put(m, at + half * D, dot_nn(trans[0], fg[:, half * W : (half + 1) * W]))
            produced(at + 2 * D)
            reserve(at + 2 * D, 2 * D)
            for m in range(2):
                cols = pl.ds(m * (FF // 2) + i * D, D)
                hg = gq.at[1]
                hg[...] = (dot_nt(fg[...], wd[cols, :]) * dgl[layer, :, cols].astype(f32)).astype(bf)
                for half in range(2):
                    put(m, at + (2 + half) * D, dot_nn(st[...], hg[:, half * W : (half + 1) * W]))
                part = dot_nt(hg[...], wu[:, cols])
                if (i, m) == (0, 0):
                    t0[...] = part
                else:
                    t0[...] += part
                s = column_sum(hg[...])
                sm[m, small_row + 9 + 2 * i : small_row + 10 + 2 * i, :] = s[:, :W]
                sm[m, small_row + 10 + 2 * i : small_row + 11 + 2 * i, :] = s[:, W:]
            produced(at + 4 * D)
        if layer == 1:
            load_weight(3, 0, True)
            load_weight(3, 0, False)
            load_weight(2, 0, True)
            load_weight(2, 0, False)
        norm_back(layer, 1, mid, t0, gn, t1, small_row)
        ag = gq.at[0]
        ag[...] = t1[...].astype(bf)
        full_row(small_row + 3, column_sum(t1[...].astype(bf)))
        if layer == 0:
            wait_weight(1, 0)
        at = row0 + 2 * RING
        trans[0] = ctx[layer].astype(bf).T
        reserve(at, D)
        for m in range(2):
            for half in range(2):
                put(
                    m, at + half * W,
                    dot_nn(trans[0, m * W : (m + 1) * W, :], ag[:, half * W : (half + 1) * W]),
                )
        produced(at + D)
        t0[...] = dot_nt(ag[...], wo[...])
        if layer == 1:
            load_weight(1, 0, True)
            load_weight(1, 0, False)
        trans[0] = nrm[layer].T
        for g in range(3):
            lanes = col128(128 * g)
            kg, qg = kf[layer, :, lanes], qf[layer, :, lanes]
            dq = dk = None
            for p in range(2):
                cols = col128(256 * g + 128 * p)
                dn = t0[:, cols] * rden[layer, :, cols]
                cx = ctx[layer, :, cols]
                vp = vv[layer, :, cols]
                dv = None
                for h in range(2):
                    i = 2 * p + h
                    a = scores(layer, g, i)
                    dn_i = (dn * two[h]).astype(bf)
                    dden = jnp.sum(dn_i.astype(f32) * cx, axis=1, keepdims=True)
                    da = ((dot_nt(dn_i, vp) - dden) * mask[...]).astype(bf)
                    v1 = dot_tn(a, dn_i)
                    q1 = dot_nn(da, kg * four[i])
                    k1 = dot_tn(da, qg * four[i])
                    dv = v1 if dv is None else dv + v1
                    dq = q1 if dq is None else dq + q1
                    dk = k1 if dk is None else dk + k1
                gq[2, :, cols] = dv.astype(bf)
            for slot, dz, sig in ((0, dq, sq), (1, dk, sk)):
                hi, lo = split_two(dz * sig[layer, :, lanes])
                dr = dot_nt(hi, pbh[layer, g]) + dot_nt(lo, pbh[layer, g]) + dot_nt(hi, pbl[layer, g])
                for p in range(2):
                    u = dr[:, 128 * p : 128 * p + 128]
                    gq[slot, :, col128(256 * g + 128 * p)] = (
                        u * cosv[...] - swap(u) * sinv[...]
                    ).astype(bf)
        if layer == 0:
            wait_weight(0, 0)
        at = row0 + 2 * RING + D
        for j in range(3):
            reserve(at + j * D, D)
            for m in range(2):
                put(m, at + j * D, dot_nn(trans[0], gq[j, :, m * W : (m + 1) * W]))
            part = dot_nt(gq[j], wq[j])
            if j == 0:
                t0[...] = part
            else:
                t0[...] += part
            s = column_sum(gq[j])
            sm[0, small_row + 6 + j : small_row + 7 + j, :] = s[:, :W]
            sm[1, small_row + 6 + j : small_row + 7 + j, :] = s[:, W:]
            produced(at + (j + 1) * D)
        if layer == 1:
            load_weight(0, 0, True)
            load_weight(0, 0, False)
        norm_back(layer, 0, X, t0, t1, gn if layer else tokens_grad, small_row)

    at = 2 * LAYER_ROWS
    rows = 16 * dp
    reserve(at, rows)
    stage[:, pl.ds(at % RING, rows), :] = jnp.zeros((2, rows, W), bf)
    for m in range(2):
        put(m, at, sm[m])
    produced(at + rows)
    while ticked[0] < K + STAGES[-1]:
        tick()
    for k in range(K):
        cb_copy(k).wait_recv()
        cb_copy(k).wait_send()
        if k >= K - 4:
            x_copy(k).wait_send()
        for i in range(Y - 1):
            y_copy(k, i).wait_send()
            yb_copy(k, i).wait_send()
        for i in range(Z - 1):
            z_copy(k, i).wait_send()
            zb_copy(k, i).wait_send()
    for u in range(G):
        for i in range(2):
            for s in range(4):
                if s != 2 or i:
                    hop(u, i, s).wait_send()


def run_main(dp, lengths, tokens, cotangent, proj, small, gains, shifts, own):
    chunks = chunks_of(dp)
    K = len(chunks)
    Y = dp // (2 * Z)
    rows = sum(size for _, size in chunks)
    slot = max(size for _, size in chunks) // 2
    G = 2 * sum(CUTS)
    dma, vm = pltpu.SemaphoreType.DMA, pltpu.VMEM
    hbm, vspec = pl.BlockSpec(memory_space=pltpu.HBM), pl.BlockSpec(memory_space=pltpu.VMEM)
    shape = jax.ShapeDtypeStruct
    out_shape = [shape((TOK, D), bf), shape((TOK, D), f32), shape((rows, W), bf)]
    out_shape += [shape(a.shape, a.dtype) for a in own]
    out_shape += [shape((2, rows // 2, W), bf), shape((rows // 2, W), bf)]
    return pl.pallas_call(
        functools.partial(main_kernel, dp, chunks),
        out_shape=out_shape,
        in_specs=[pl.BlockSpec(memory_space=pltpu.SMEM)] + [vspec] * 6 + [hbm] * 4,
        out_specs=[vspec, vspec] + [hbm] * 7,
        scratch_shapes=[
            vm((16, W), f32),
            vm((3, D, D), bf), vm((D, D), bf), vm((D, FF), bf), vm((FF, D), bf),
            vm((2, TOK, D), f32), vm((2, TOK, D), f32), vm((2, TOK, D), bf), vm((2, TOK, D), bf),
            vm((2, TOK, W), bf), vm((2, TOK, W), bf), vm((2, TOK, W), f32), vm((2, TOK, W), f32),
            vm((2, TOK, D), bf), vm((2, TOK, D), f32), vm((2, TOK, D), f32),
            vm((2, TOK, FF), bf), vm((2, TOK, FF), bf),
            vm((2, 3, 256, 128), bf), vm((2, 3, 256, 128), bf),
            vm((TOK, TOK), f32), vm((TOK, 128), f32), vm((TOK, 128), f32),
            vm((TOK, D), f32), vm((TOK, D), f32), vm((TOK, D), f32), vm((TOK, D), f32),
            vm((3, TOK, D), bf), vm((2, D, TOK), bf), vm((2, 32, W), f32),
            vm((2, RING, W), bf), vm((rows // 2, W), bf),
            vm((4, slot, W), bf), vm((2, slot, W), bf), vm((slot, W), bf),
            vm((rows // (2 * Y) * (Y - 1), W), bf), vm((rows // (2 * Y * Z) * (Z - 1), W), bf),
            dma((G + 1, 8)), dma((G + 1, 8)), dma((7, 2)),
            dma((K,)), dma((K,)), dma((1,)), dma((K,)), dma((K,)), dma((1,)),
            dma((K, Y - 1)), dma((K, Y - 1)),
            dma((K, Z - 1)), dma((K, Z - 1)),
            dma((K, Z - 1)), dma((K, Z - 1)),
            dma((K, Y - 1)), dma((K, Y - 1)),
            dma((K,)), dma((K,)), dma((K,)),
        ],
        compiler_params=pltpu.CompilerParams(
            collective_id=0, has_side_effects=True, vmem_limit_bytes=64 * 2**20
        ),
        name="layers",
    )(lengths, tokens, cotangent, proj, small, gains, shifts, *own)


def on_device(
    dp, tokens, cotangent, lengths, random_proj, attn_weight, attn_bias, out_weight, norm_gains,
    biases, up_weight, up_bias, down_weight,
):
    small = jnp.concatenate(
        [attn_bias.reshape(6, W), up_bias.reshape(8, W), jnp.zeros((2, W), bf)]
    ).astype(f32)
    own = (attn_weight.reshape(2, 3 * D, W), out_weight, up_weight, down_weight)
    result = run_main(
        dp, lengths, tokens, cotangent, random_proj.reshape(2, HEADS * HD, FEATS), small,
        norm_gains.reshape(4, D).astype(f32), biases.reshape(8, D).astype(f32), own,
    )
    stack_out, tokens_grad, reduced = result[:3]

    def columns(block, count):
        return jnp.concatenate(jnp.split(block, count), axis=1)

    big = [[], [], [], []]
    for layer in range(2):
        at = (1 - layer) * LAYER_ROWS
        down, up = [], []
        for i in range(2):
            down.append(columns(reduced[at + i * RING : at + i * RING + 2 * D], 2))
            up.append(columns(reduced[at + i * RING + 2 * D : at + (i + 1) * RING], 2))
        at += 2 * RING
        big[0].append(reduced[at + D : at + 4 * D].reshape(3, D, W))
        big[1].append(columns(reduced[at : at + D], 2))
        big[2].append(jnp.concatenate(up, axis=1))
        big[3].append(jnp.concatenate(down))
    attn_g, out_g, up_g, down_g = [jnp.stack(v).astype(f32) for v in big]
    rest = reduced[2 * LAYER_ROWS : 2 * LAYER_ROWS + 26].astype(f32).reshape(2, 13, W)[::-1]
    return (
        stack_out, tokens_grad, attn_g, rest[:, 6:9], out_g, rest[:, :2], rest[:, 2:6], up_g,
        rest[:, 9:13].reshape(2, FF // 2), down_g,
    )


def solution(mesh):
    return jax.shard_map(
        functools.partial(on_device, mesh.shape["dp"]),
        mesh=mesh,
        in_specs=(
            P(("dp", "mp"), None), P(("dp", "mp"), None), P(("dp", "mp"), None), P(),
            P(None, None, None, "mp"), P(None, None, "mp"), P(None, "mp", None), P(), P(),
            P(None, None, "mp"), P(None, "mp"), P(None, "mp", None),
        ),
        out_specs=(
            P(("dp", "mp"), None), P(("dp", "mp"), None), P(None, None, None, "mp"),
            P(None, None, "mp"), P(None, "mp", None), P(None, None, "mp"), P(None, None, "mp"),
            P(None, None, "mp"), P(None, "mp"), P(None, "mp", None),
        ),
        check_vma=False,
    )
```

```python
import functools
import math

import jax
import jax.numpy as jnp
from jax import lax
from jax.experimental import pallas as pl
from jax.experimental.pallas import tpu as pltpu
from jax.sharding import PartitionSpec as P

MESH = pl.DeviceIdType.MESH
f32, bf = jnp.float32, jnp.bfloat16
TOK, D, HEADS, HD, FEATS = 256, 768, 12, 64, 32
W = D // 2
FF = 4 * D
RING = 4 * D
LAYER_ROWS = 12 * D
LAG = 2
STAGES = [1, 4, 6, 8, 10, 12]
CUTS = (((1,), (1,), (2, 2), (2, 2)), ((1,), (1,), (2, 2), (2, 4, 4)))
Z = 4


def rdma(src, dst, send, recv, dev):
    return pltpu.make_async_remote_copy(
        src_ref=src, dst_ref=dst, send_sem=send, recv_sem=recv, device_id=dev, device_id_type=MESH
    )


def dot_nn(a, b):
    return jnp.dot(a, b, preferred_element_type=f32)


def dot_nt(a, b):
    return lax.dot_general(a, b, (((1,), (1,)), ((), ())), preferred_element_type=f32)


def dot_tn(a, b):
    return lax.dot_general(a, b, (((0,), (0,)), ((), ())), preferred_element_type=f32)


def split_two(v):
    high = v.astype(bf)
    return high, (v - high.astype(f32)).astype(bf)


def al(v, m=16):
    return pl.multiple_of(v, m)


def chunks_of(dp):
    step = D if dp <= 16 else 16 * dp
    out = [(at, step) for at in range(0, 2 * LAYER_ROWS, step)]
    if step > 16 * dp:
        at, size = out.pop()
        out += [(r, 16 * dp) for r in range(at, at + size, 16 * dp)]
    return out + [(2 * LAYER_ROWS, 16 * dp)]


def gather_groups(rows):
    groups = []
    for layer in range(2):
        for t in range(4):
            at = 0
            for share in CUTS[layer][t]:
                size = rows[t] // share
                third = size // 3
                groups.append(
                    [(layer, t, at, third, False), (layer, t, at + third, size - third, True)]
                )
                at += size
    return groups


def rows_loop(body, tile, init=0):
    def step(i, carry):
        return body(pl.ds(al(i * tile, tile), tile), carry)

    return lax.fori_loop(0, TOK // tile, step, init)


def fold(v):
    return jnp.sum(v.reshape(v.shape[0] // 8, 8, v.shape[1]), axis=0)


def main_kernel(
    dp, chunks,
    lengths, tokens, cotangent, proj, attn_bias, up_bias, gains, shifts,
    own_a, own_o, own_u, own_d,
    stack_out, tokens_grad, reduced, oth_a, oth_o, oth_u, oth_d, cland, xland,
    own_small, oth_small, wq, wo, wu, wd,
    X, mid, nrm, sec, qf, kf, sq, sk, vv, rden, ctx, act, dgl,
    pbh, pbl, mask, cosv, sinv, t0, t1, t2, gn, gq, trans, sm,
    stage, acc, xsend, cslot, xslot, ybuf, zbuf,
    gs, gr, wsem, lsem, cs, cr, cl, xs, xr, xl, ys, yr, zs, zr, bs, br, as_, ar, es, er, os,
):
    Y = dp // (2 * Z)
    d, x = lax.axis_index("dp"), lax.axis_index("mp")
    core = d % 2
    yy, zz = (d // 2) % Y, d // (2 * Y)
    ys_peer = [(yy + i) % Y for i in range(1, Y)]
    zs_peer = [(zz + i) % Z for i in range(1, Z)]
    to_x = (d, 1 - x)
    to_core = (d + 1 - 2 * core, x)
    to_y = [((zz * Y + p) * 2 + core, x) for p in ys_peer]
    to_z = [((p * Y + yy) * 2 + core, x) for p in zs_peer]
    peers = [to_core, to_x] + to_y + to_z
    barrier = pltpu.get_barrier_semaphore()
    own_small[...] = jnp.zeros_like(own_small)
    for layer in range(2):
        own_small[3 * layer : 3 * layer + 3, :] = attn_bias[layer].astype(f32)
        row = up_bias[layer : layer + 1, :].astype(f32)
        for i in range(4):
            own_small[6 + 4 * layer + i : 7 + 4 * layer + i, :] = row[:, i * W : (i + 1) * W]
    for peer in peers:
        pl.semaphore_signal(barrier, inc=1, device_id=peer, device_id_type=MESH)
    pl.semaphore_wait(barrier, len(peers))

    own = (own_a, own_o, own_u, own_d)
    oth = (oth_a, oth_o, oth_u, oth_d)
    y1, z1 = (d // 2) % 2, (d // 4) % 2
    gather_y = (d + 2 - 4 * y1, x)
    gather_z = (d + 4 - 8 * z1, x)
    groups = gather_groups([r.shape[1] for r in own])
    G = len(groups)

    def hop(u, i, stage_):
        layer, t, first, rows, wide = groups[u][i]
        piece = rows // (8 if wide else 4)
        base = first + core * (rows // 2)
        src = oth[t]
        if stage_ == 0:
            start = base + (z1 * 2 + y1 if wide else y1) * piece
            size, dev, src = piece, to_x, own[t]
        elif stage_ == 1:
            start = base + (z1 * 2 + y1 if wide else y1) * piece
            size, dev = piece, gather_y
        elif stage_ == 2:
            start, size, dev = base + z1 * 2 * piece, 2 * piece, gather_z
        else:
            start, size, dev = base, rows // 2, to_core
        return rdma(
            src.at[layer, pl.ds(al(start), size)],
            oth[t].at[layer, pl.ds(al(start), size)],
            gs.at[u, 4 * i + stage_],
            gr.at[u, 4 * i + stage_],
            dev,
        )

    small_copy = rdma(own_small, oth_small, gs.at[G, 0], gr.at[G, 0], to_x)
    small_copy.start()
    for u in range(G):
        hop(u, 0, 0).start()
        hop(u, 1, 0).start()
    pumped = [0]

    def pump(count):
        for step in range(pumped[0], min(pumped[0] + count, G + 2 * LAG)):
            u = step - 2 * LAG
            if 0 <= u < G:
                hop(u, 1, 2).wait_recv()
                hop(u, 1, 3).start()
            u = step - LAG
            if 0 <= u < G:
                hop(u, 1, 1).wait_recv()
                hop(u, 1, 2).start()
                hop(u, 0, 1).wait_recv()
                hop(u, 0, 3).start()
            u = step
            if u < G:
                hop(u, 1, 0).wait_recv()
                hop(u, 1, 1).start()
                hop(u, 0, 0).wait_recv()
                hop(u, 0, 1).start()
            pumped[0] = step + 1

    def weight_copies(t, layer, mine):
        src = (own if mine else oth)[t].at[layer]
        m = 0 if mine else 1
        sem = wsem.at[t, m]
        if t == 0:
            return [
                pltpu.make_async_copy(
                    src.at[pl.ds(j * D, D)], wq.at[j, :, pl.ds(m * W, W)], wsem.at[4 + j, m]
                )
                for j in range(3)
            ]
        if t == 1:
            return [pltpu.make_async_copy(src, wo.at[pl.ds(m * W, W)], sem)]
        if t == 2:
            return [pltpu.make_async_copy(src, wu.at[:, pl.ds(m * (FF // 2), FF // 2)], sem)]
        return [pltpu.make_async_copy(src, wd.at[pl.ds(m * (FF // 2), FF // 2)], sem)]

    def load_weight(t, layer, mine):
        for c in weight_copies(t, layer, mine):
            c.start()

    def wait_weight(t, layer, halves=(True, False)):
        for mine in halves:
            for c in weight_copies(t, layer, mine):
                c.wait()

    def late_copies(u):
        layer, t, first, size, _ = groups[u][0]
        size += groups[u][1][3]
        src = oth[t].at[layer, pl.ds(first, size)]
        if t == 0:
            return weight_copies(0, layer, False)
        if t == 1:
            return weight_copies(1, layer, False)
        if t == 2:
            dst = wu.at[pl.ds(first, size), pl.ds(FF // 2, FF // 2)]
        else:
            dst = wd.at[pl.ds(FF // 2 + first, size)]
        return [pltpu.make_async_copy(src, dst, lsem.at[u])]

    def late_groups(t, layer, parts):
        found = [u for u in range(G) if groups[u][0][:2] == (layer, t)]
        return found if parts is None else [found[p] for p in parts]

    def arrived(t, layer, parts=None):
        for u in late_groups(t, layer, parts):
            hop(u, 0, 3).wait_recv()
            hop(u, 1, 3).wait_recv()
            for c in late_copies(u):
                c.start()

    def wait_late(t, layer, parts=None):
        for u in late_groups(t, layer, parts):
            for c in late_copies(u):
                c.wait()

    K = len(chunks)
    slot_rows = max(size for _, size in chunks) // 2

    def sizes(k):
        at, rows = chunks[k]
        return at, rows, rows // 2, rows // 2 // Y, rows // 2 // Y // Z

    def core_copy(k):
        at, rows, half, _, _ = sizes(k)
        return rdma(
            stage.at[:, pl.ds(al(at % RING + (1 - core) * half), half)],
            cland.at[:, pl.ds(at // 2, half)],
            cs.at[k], cr.at[k], to_core,
        )

    def core_load(k):
        at, rows, half, _, _ = sizes(k)
        return pltpu.make_async_copy(
            cland.at[:, pl.ds(at // 2, half)], cslot.at[:, pl.ds(0, half)], cl.at[0]
        )

    def x_copy(k):
        at, rows, half, _, _ = sizes(k)
        return rdma(
            xsend.at[k % 4, pl.ds(0, half)], xland.at[pl.ds(at // 2, half)], xs.at[k], xr.at[k], to_x
        )

    def x_load(k):
        at, rows, half, _, _ = sizes(k)
        return pltpu.make_async_copy(
            xland.at[pl.ds(at // 2, half)], xslot.at[pl.ds(0, half)], xl.at[0]
        )

    def y_copy(k, i):
        at, rows, half, quarter, _ = sizes(k)
        base = at // (2 * Y) * (Y - 1)
        return rdma(
            acc.at[pl.ds(al(at // 2 + ys_peer[i] * quarter), quarter)],
            ybuf.at[pl.ds(base + i * quarter, quarter)],
            ys.at[k, i], yr.at[k, i], to_y[i],
        )

    def z_copy(k, i):
        at, rows, half, quarter, piece = sizes(k)
        base = at // (2 * Y * Z) * (Z - 1)
        return rdma(
            acc.at[pl.ds(al(at // 2 + yy * quarter + zs_peer[i] * piece), piece)],
            zbuf.at[pl.ds(base + i * piece, piece)],
            zs.at[k, i], zr.at[k, i], to_z[i],
        )

    def mine_rows(k):
        at, rows, half, quarter, piece = sizes(k)
        return (
            pl.ds(al(at // 2 + yy * quarter + zz * piece), piece),
            pl.ds(al(at + core * half + yy * quarter + zz * piece), piece),
        )

    def own_copy(k):
        a, b = mine_rows(k)
        return pltpu.make_async_copy(acc.at[a], reduced.at[b], os.at[k])

    def zb_copy(k, i):
        a, b = mine_rows(k)
        return rdma(acc.at[a], reduced.at[b], bs.at[k, i], br.at[k, i], to_z[i])

    def yb_copy(k, i):
        at, rows, half, quarter, piece = sizes(k)
        r = pl.ds(al(at + core * half + yy * quarter), quarter)
        return rdma(reduced.at[r], reduced.at[r], as_.at[k, i], ar.at[k, i], to_y[i])

    def cb_copy(k):
        at, rows, half, quarter, piece = sizes(k)
        r = pl.ds(al(at + core * half), half)
        return rdma(reduced.at[r], reduced.at[r], es.at[k], er.at[k], to_core)

    def add_rows(total, dst, dst_at, srcs):
        tile = 16
        for size in (128, 96, 64, 48, 32):
            if total % size == 0:
                tile = size
                break

        def body(i, carry):
            r0 = i * tile
            v = None
            for ref, at in srcs:
                part = ref[pl.ds(al(at + r0), tile)].astype(f32)
                v = part if v is None else v + part
            dst[pl.ds(al(dst_at + r0), tile)] = v.astype(bf)
            return carry

        lax.fori_loop(0, total // tile, body, 0)

    def s1(k):
        at, rows, half, quarter, piece = sizes(k)
        core_copy(k).wait_recv()
        core_load(k).start()
        if k >= 4:
            x_copy(k - 4).wait_send()
        core_load(k).wait()
        here = at % RING + core * half
        add_rows(half, xsend.at[k % 4], 0, [(stage.at[1], here), (cslot.at[1], 0)])
        x_copy(k).start()
        add_rows(half, acc, at // 2, [(stage.at[0], here), (cslot.at[0], 0)])

    def s2(k):
        at, rows, half, quarter, piece = sizes(k)
        x_copy(k).wait_recv()
        x_load(k).start()
        x_load(k).wait()
        add_rows(half, acc, at // 2, [(acc, at // 2), (xslot, 0)])
        for i in range(Y - 1):
            y_copy(k, i).start()

    def s3(k):
        at, rows, half, quarter, piece = sizes(k)
        base = at // (2 * Y) * (Y - 1)
        for i in range(Y - 1):
            y_copy(k, i).wait_recv()
        here = at // 2 + yy * quarter
        add_rows(quarter, acc, here, [(acc, here)] + [(ybuf, base + i * quarter) for i in range(Y - 1)])
        for i in range(Z - 1):
            z_copy(k, i).start()

    def s4(k):
        at, rows, half, quarter, piece = sizes(k)
        base = at // (2 * Y * Z) * (Z - 1)
        for i in range(Z - 1):
            z_copy(k, i).wait_recv()
        here = at // 2 + yy * quarter + zz * piece
        add_rows(piece, acc, here, [(acc, here)] + [(zbuf, base + i * piece) for i in range(Z - 1)])
        own_copy(k).start()
        for i in range(Z - 1):
            zb_copy(k, i).start()

    def s5(k):
        own_copy(k).wait()
        for i in range(Z - 1):
            zb_copy(k, i).wait_recv()
        for i in range(Y - 1):
            yb_copy(k, i).start()

    def s6(k):
        for i in range(Y - 1):
            yb_copy(k, i).wait_recv()
        cb_copy(k).start()

    ticked = [0]
    settled = [0]

    def settle(k):
        while settled[0] <= k:
            s1(settled[0])
            core_copy(settled[0]).wait_send()
            settled[0] += 1

    def tick():
        t = ticked[0]
        ticked[0] += 1
        for fn, off in reversed(list(zip([s2, s3, s4, s5, s6], STAGES[1:]))):
            if 0 <= t - off < K:
                fn(t - off)
        if 0 <= t - STAGES[0] < K:
            settle(t - STAGES[0])

    made = [0]

    def reserve(start, size):
        assert all(settled[0] > k for k in range(K) if chunks[k][0] < start + size - RING)

    def produced(upto):
        made[0] = upto
        while ticked[0] < K and chunks[ticked[0]][0] + chunks[ticked[0]][1] <= upto:
            core_copy(ticked[0]).start()
            tick()

    for t in range(4):
        load_weight(t, 0, True)
    row_i = lax.broadcasted_iota(jnp.int32, (TOK, 128), 0)
    lane = lax.broadcasted_iota(jnp.int32, (TOK, 128), 1)
    lane_row = lax.broadcasted_iota(jnp.int32, (1, 128), 1)
    seg_r = jnp.zeros((TOK, 1), jnp.int32)
    seg_c = jnp.zeros((1, TOK), jnp.int32)
    begin = jnp.zeros((TOK, 128), jnp.int32)
    r1 = lax.broadcasted_iota(jnp.int32, (TOK, 1), 0)
    c1 = lax.broadcasted_iota(jnp.int32, (1, TOK), 1)
    finish = jnp.int32(0)
    for i in range(8):
        size = lengths[0, i]
        finish = finish + size
        seg_r = seg_r + jnp.where(r1 >= finish, 1, 0)
        seg_c = seg_c + jnp.where(c1 >= finish, 1, 0)
        begin = begin + jnp.where(row_i >= finish, size, 0)
    mask[...] = jnp.where(seg_r == seg_c, 1.0, 0.0).astype(f32)
    place = (row_i - begin).astype(f32)
    freq = jnp.exp((lane % (HD // 2)).astype(f32) * (-2.0 * math.log(10000.0) / HD))
    angle = place * freq
    low_half = (lane % HD) < (HD // 2)
    cosv[...] = jnp.cos(angle)
    sn = jnp.sin(angle)
    sinv[...] = jnp.where(low_half, -sn, sn)
    low_row = (lane_row % HD) < (HD // 2)
    four = [jnp.where(lane_row // FEATS == i, 1.0, 0.0).astype(bf) for i in range(4)]
    two = [jnp.where(lane_row // HD == i, 1.0, 0.0).astype(f32) for i in range(2)]

    block_row = lax.broadcasted_iota(jnp.int32, (128, 256), 0) // FEATS
    block_col = lax.broadcasted_iota(jnp.int32, (128, 256), 1) // HD
    diag = jnp.where(block_row == block_col, HD ** -0.25, 0.0).astype(f32)
    for layer in range(2):
        for g in range(3):
            pieces = []
            for i in range(4):
                h = 4 * g + i
                first = x if h < 6 else 1 - x
                pieces.append(proj[layer, first * (HEADS // 2) + h % (HEADS // 2)])
            p = jnp.concatenate(pieces, axis=0)
            p = jnp.concatenate([p] * 4, axis=1) * diag
            hi, lo = split_two(p)
            pbh[layer, g] = hi
            pbl[layer, g] = lo

    def swap(u):
        return jnp.where(low_row, pltpu.roll(u, 96, 1), pltpu.roll(u, 32, 1))

    def col128(at):
        return pl.ds(at, 128)

    def up_bias_row(layer, m, i):
        src = own_small if m == 0 else oth_small
        r = 6 + 4 * layer + 2 * i
        return jnp.concatenate([src[r : r + 1, :], src[r + 1 : r + 2, :]], axis=1)

    def gain(layer, i):
        return gains[layer].astype(f32)[i : i + 1, :]

    def shift(layer, i):
        return shifts[layer].astype(f32)[i : i + 1, :]

    def norm_into(src, layer, i, dst):
        g, b = gain(layer, i), shift(layer, 2 * i)

        def body(rows, carry):
            v = src[layer, rows, :]
            c = v - jnp.mean(v, axis=-1, keepdims=True)
            r = lax.rsqrt(jnp.mean(c * c, axis=-1, keepdims=True) + 1e-05)
            dst[layer, rows, :] = (c * r * g + b).astype(bf)
            return carry

        rows_loop(body, 32)

    def project(layer, m):
        src = own_small if m == 0 else oth_small
        cols = pl.ds(m * W, W)
        for j, dst in enumerate((t0, t1, vv.at[layer])):
            row = 3 * layer + j
            dst[:, cols] = (dot_nn(nrm[layer], wq[j, :, cols]) + src[row : row + 1, :]).astype(dst.dtype)

    def feature(src, layer, g, feat, sig):
        parts = []
        for p in range(2):
            u = src[:, col128(256 * g + 128 * p)]
            parts.append(u * cosv[...] + swap(u) * sinv[...])
        hi, lo = split_two(jnp.concatenate(parts, axis=1))
        z = dot_nt(hi, pbh[layer, g]) + dot_nt(lo, pbh[layer, g]) + dot_nt(hi, pbl[layer, g])
        f = jnp.maximum(z, 0.0) + jnp.log1p(jnp.exp(-jnp.abs(z)))
        feat[layer, :, col128(128 * g)] = f.astype(bf)
        sig[layer, :, col128(128 * g)] = jnp.exp(z - f)

    def scores(layer, g, i):
        q = qf[layer, :, col128(128 * g)] * four[i]
        return (dot_nt(q, kf[layer, :, col128(128 * g)]) * mask[...]).astype(bf)

    def attention(layer, g):
        feature(t0, layer, g, qf, sq)
        feature(t1, layer, g, kf, sk)
        ones = jnp.ones((TOK, 128), bf)
        for p in range(2):
            cols = col128(256 * g + 128 * p)
            right = jnp.concatenate([vv[layer, :, cols], ones], axis=1)
            a = dot_nn(scores(layer, g, 2 * p), right)
            b = dot_nn(scores(layer, g, 2 * p + 1), right)
            first = lane_row < HD
            num = jnp.where(first, a[:, :128], b[:, :128])
            den = jnp.where(first, a[:, 128:], b[:, 128:])
            r = 1.0 / den
            rden[layer, :, cols] = r
            ctx[layer, :, cols] = num * r

    def out_project(layer):
        mid[layer] = X[layer] + dot_nn(ctx[layer].astype(bf), wo[...]) + shift(layer, 1)
        norm_into(mid, layer, 1, sec)

    def feed(layer, m, i):
        cols = pl.ds(m * (FF // 2) + i * D, D)
        t0[...] = dot_nn(sec[layer], wu[:, cols])
        b = up_bias_row(layer, m, i)

        def body(rows, carry):
            h = t0[rows, :] + b
            phi = 0.5 + 0.5 * lax.erf(h * (2.0 ** -0.5))
            act[layer, rows, cols] = (h * phi).astype(bf)
            dgl[layer, rows, cols] = (
                phi + h * (jnp.exp(-0.5 * h * h) * ((2.0 * math.pi) ** -0.5))
            ).astype(bf)
            return carry

        rows_loop(body, 16)
        part = dot_nn(act[layer, :, cols], wd[cols, :])
        if (m, i) == (0, 0):
            t2[...] = part + mid[layer] + shift(layer, 3)
        else:
            t2[...] += part

    X[0] = tokens[...].astype(f32)
    norm_into(X, 0, 0, nrm)
    wait_weight(0, 0, (True,))
    pump(1)
    project(0, 0)
    pump(1)
    attention(0, 0)
    pump(4)
    arrived(0, 0)
    small_copy.wait()
    wait_late(0, 0)
    project(0, 1)
    load_weight(0, 1, True)
    pump(1)
    attention(0, 1)
    attention(0, 2)
    arrived(1, 0)
    pump(1)
    wait_weight(1, 0, (True,))
    wait_late(1, 0)
    out_project(0)
    load_weight(1, 1, True)
    pump(1)
    arrived(2, 0)
    wait_weight(2, 0, (True,))
    wait_weight(3, 0, (True,))
    feed(0, 0, 0)
    pump(1)
    feed(0, 0, 1)
    arrived(3, 0, (0,))
    wait_late(2, 0)
    wait_late(3, 0, (0,))
    pump(1)
    feed(0, 1, 0)
    arrived(3, 0, (1,))
    pump(1)
    wait_late(3, 0, (1,))
    feed(0, 1, 1)
    load_weight(2, 1, True)
    load_weight(3, 1, True)
    arrived(0, 1)
    X[1] = t2[...]
    norm_into(X, 1, 0, nrm)
    pump(1)
    arrived(1, 1)
    wait_weight(0, 1, (True,))
    wait_late(0, 1)
    project(1, 0)
    attention(1, 0)
    pump(1)
    project(1, 1)
    attention(1, 1)
    pump(1)
    attention(1, 2)
    wait_weight(1, 1, (True,))
    wait_late(1, 1)
    out_project(1)
    pump(1)
    wait_weight(2, 1, (True,))
    wait_weight(3, 1, (True,))
    feed(1, 0, 0)
    pump(1)
    arrived(2, 1)
    arrived(3, 1, (0,))
    feed(1, 0, 1)
    wait_late(2, 1)
    wait_late(3, 1, (0,))
    feed(1, 1, 0)
    arrived(3, 1, (1, 2))
    wait_late(3, 1, (1, 2))
    feed(1, 1, 1)
    stack_out[...] = t2[...].astype(bf)

    sm[...] = jnp.zeros_like(sm)

    def full_row(row, v):
        first, second = v[:, :W], v[:, W:]
        sm[0, row : row + 1, :] = jnp.where(x == 0, first, second)
        sm[1, row : row + 1, :] = jnp.where(x == 0, second, first)

    def norm_back(layer, i, src, up, base, dst, base_row):
        g = gain(layer, i)
        zero = jnp.zeros((8, D), f32)

        def body(rows, carry):
            v = src[layer, rows, :]
            u = up[rows, :]
            c = v - jnp.mean(v, axis=-1, keepdims=True)
            r = lax.rsqrt(jnp.mean(c * c, axis=-1, keepdims=True) + 1e-05)
            hat = c * r
            dh = u * g
            dv = r * (
                dh
                - jnp.mean(dh, axis=-1, keepdims=True)
                - hat * jnp.mean(dh * hat, axis=-1, keepdims=True)
            )
            dst[rows, :] = base[rows, :] + dv
            return (carry[0] + fold(u * hat), carry[1] + fold(u))

        a, b = rows_loop(body, 32, (zero, zero))
        full_row(base_row + i, jnp.sum(a, axis=0, keepdims=True))
        full_row(base_row + 2 + 2 * i, jnp.sum(b, axis=0, keepdims=True))

    def column_sum(v):
        return jnp.sum(v.astype(f32), axis=0, keepdims=True)

    def put(m, row, v):
        stage[m, pl.ds(row % RING, v.shape[0]), :] = v.astype(bf)

    gn[...] = cotangent[...].astype(f32)
    for layer in (1, 0):
        row0 = (1 - layer) * LAYER_ROWS
        small_row = (1 - layer) * 13
        if layer == 0:
            wait_weight(3, 0)
            wait_weight(2, 0)
        fg = gq.at[0]
        fg[...] = gn[...].astype(bf)
        full_row(small_row + 5, column_sum(gn[...].astype(bf)))
        st = trans.at[1]
        st[...] = sec[layer].T
        for i in range(2):
            at = row0 + i * RING
            for half in range(2):
                reserve(at + half * D, D)
                for m in range(2):
                    if half == 0:
                        cols = pl.ds(m * (FF // 2) + i * D, D)
                        trans[2 * m] = act[layer, :, cols].T
                    put(m, at + half * D, dot_nn(trans[2 * m], fg[:, half * W : (half + 1) * W]))
                produced(at + (half + 1) * D)
            reserve(at + 2 * D, 2 * D)
            for m in range(2):
                cols = pl.ds(m * (FF // 2) + i * D, D)
                hg = gq.at[1]
                hg[...] = (dot_nt(fg[...], wd[cols, :]) * dgl[layer, :, cols].astype(f32)).astype(bf)
                for half in range(2):
                    put(m, at + (2 + half) * D, dot_nn(st[...], hg[:, half * W : (half + 1) * W]))
                part = dot_nt(hg[...], wu[:, cols])
                if (i, m) == (0, 0):
                    t0[...] = part
                else:
                    t0[...] += part
                s = column_sum(hg[...])
                sm[m, small_row + 9 + 2 * i : small_row + 10 + 2 * i, :] = s[:, :W]
                sm[m, small_row + 10 + 2 * i : small_row + 11 + 2 * i, :] = s[:, W:]
            produced(at + 4 * D)
        if layer == 1:
            load_weight(3, 0, True)
            load_weight(3, 0, False)
            load_weight(2, 0, True)
            load_weight(2, 0, False)
        norm_back(layer, 1, mid, t0, gn, t1, small_row)
        ag = gq.at[0]
        ag[...] = t1[...].astype(bf)
        full_row(small_row + 3, column_sum(t1[...].astype(bf)))
        if layer == 0:
            wait_weight(1, 0)
        at = row0 + 2 * RING
        trans[0] = ctx[layer].astype(bf).T
        reserve(at, D)
        for m in range(2):
            for half in range(2):
                put(
                    m, at + half * W,
                    dot_nn(trans[0, m * W : (m + 1) * W, :], ag[:, half * W : (half + 1) * W]),
                )
        produced(at + D)
        t0[...] = dot_nt(ag[...], wo[...])
        if layer == 1:
            load_weight(1, 0, True)
            load_weight(1, 0, False)
        trans[0] = nrm[layer].T
        for g in range(3):
            lanes = col128(128 * g)
            kg, qg = kf[layer, :, lanes], qf[layer, :, lanes]
            dq = dk = None
            for p in range(2):
                cols = col128(256 * g + 128 * p)
                dn = t0[:, cols] * rden[layer, :, cols]
                cx = ctx[layer, :, cols]
                vp = vv[layer, :, cols]
                dv = None
                for h in range(2):
                    i = 2 * p + h
                    a = scores(layer, g, i)
                    dn_i = (dn * two[h]).astype(bf)
                    dden = jnp.sum(dn_i.astype(f32) * cx, axis=1, keepdims=True)
                    da = ((dot_nt(dn_i, vp) - dden) * mask[...]).astype(bf)
                    v1 = dot_tn(a, dn_i)
                    q1 = dot_nn(da, kg * four[i])
                    k1 = dot_tn(da, qg * four[i])
                    dv = v1 if dv is None else dv + v1
                    dq = q1 if dq is None else dq + q1
                    dk = k1 if dk is None else dk + k1
                gq[2, :, cols] = dv.astype(bf)
            for slot, dz, sig in ((0, dq, sq), (1, dk, sk)):
                hi, lo = split_two(dz * sig[layer, :, lanes])
                dr = dot_nn(hi, pbh[layer, g]) + dot_nn(lo, pbh[layer, g]) + dot_nn(hi, pbl[layer, g])
                for p in range(2):
                    u = dr[:, 128 * p : 128 * p + 128]
                    gq[slot, :, col128(256 * g + 128 * p)] = (
                        u * cosv[...] - swap(u) * sinv[...]
                    ).astype(bf)
        if layer == 0:
            wait_weight(0, 0)
        at = row0 + 2 * RING + D
        for j in range(3):
            reserve(at + j * D, D)
            for m in range(2):
                put(m, at + j * D, dot_nn(trans[0], gq[j, :, m * W : (m + 1) * W]))
            part = dot_nt(gq[j], wq[j])
            if j == 0:
                t0[...] = part
            else:
                t0[...] += part
            s = column_sum(gq[j])
            sm[0, small_row + 6 + j : small_row + 7 + j, :] = s[:, :W]
            sm[1, small_row + 6 + j : small_row + 7 + j, :] = s[:, W:]
            produced(at + (j + 1) * D)
        if layer == 1:
            load_weight(0, 0, True)
            load_weight(0, 0, False)
        norm_back(layer, 0, X, t0, t1, gn if layer else tokens_grad, small_row)

    at = 2 * LAYER_ROWS
    rows = 16 * dp
    reserve(at, rows)
    stage[:, pl.ds(at % RING, rows), :] = jnp.zeros((2, rows, W), bf)
    for m in range(2):
        put(m, at, sm[m])
    produced(at + rows)
    while ticked[0] < K + STAGES[-1]:
        tick()
    for k in range(K):
        cb_copy(k).wait_recv()
        cb_copy(k).wait_send()
        if k >= K - 4:
            x_copy(k).wait_send()
        for i in range(Y - 1):
            y_copy(k, i).wait_send()
            yb_copy(k, i).wait_send()
        for i in range(Z - 1):
            z_copy(k, i).wait_send()
            zb_copy(k, i).wait_send()
    for u in range(G):
        for i in range(2):
            for s in range(4):
                if s != 2 or i:
                    hop(u, i, s).wait_send()


def run_main(dp, lengths, tokens, cotangent, proj, attn_bias, up_bias, gains, shifts, own):
    chunks = chunks_of(dp)
    K = len(chunks)
    Y = dp // (2 * Z)
    rows = sum(size for _, size in chunks)
    slot = max(size for _, size in chunks) // 2
    G = sum(len(c) for layer in CUTS for c in layer)
    dma, vm = pltpu.SemaphoreType.DMA, pltpu.VMEM
    hbm, vspec = pl.BlockSpec(memory_space=pltpu.HBM), pl.BlockSpec(memory_space=pltpu.VMEM)
    shape = jax.ShapeDtypeStruct
    out_shape = [shape((TOK, D), bf), shape((TOK, D), f32), shape((rows, W), bf)]
    out_shape += [shape(a.shape, a.dtype) for a in own]
    out_shape += [shape((2, rows // 2, W), bf), shape((rows // 2, W), bf)]
    return pl.pallas_call(
        functools.partial(main_kernel, dp, chunks),
        out_shape=out_shape,
        in_specs=[pl.BlockSpec(memory_space=pltpu.SMEM)] + [vspec] * 7 + [hbm] * 4,
        out_specs=[vspec, vspec] + [hbm] * 7,
        scratch_shapes=[
            vm((16, W), f32), vm((16, W), f32),
            vm((3, D, D), bf), vm((D, D), bf), vm((D, FF), bf), vm((FF, D), bf),
            vm((2, TOK, D), f32), vm((2, TOK, D), f32), vm((2, TOK, D), bf), vm((2, TOK, D), bf),
            vm((2, TOK, W), bf), vm((2, TOK, W), bf), vm((2, TOK, W), f32), vm((2, TOK, W), f32),
            vm((2, TOK, D), bf), vm((2, TOK, D), f32), vm((2, TOK, D), f32),
            vm((2, TOK, FF), bf), vm((2, TOK, FF), bf),
            vm((2, 3, 128, 256), bf), vm((2, 3, 128, 256), bf),
            vm((TOK, TOK), f32), vm((TOK, 128), f32), vm((TOK, 128), f32),
            vm((TOK, D), f32), vm((TOK, D), f32), vm((TOK, D), f32), vm((TOK, D), f32),
            vm((3, TOK, D), bf), vm((3, D, TOK), bf), vm((2, 32, W), f32),
            vm((2, RING, W), bf), vm((rows // 2, W), bf),
            vm((4, slot, W), bf), vm((2, slot, W), bf), vm((slot, W), bf),
            vm((rows // (2 * Y) * (Y - 1), W), bf), vm((rows // (2 * Y * Z) * (Z - 1), W), bf),
            dma((G + 1, 8)), dma((G + 1, 8)), dma((7, 2)), dma((G,)),
            dma((K,)), dma((K,)), dma((1,)), dma((K,)), dma((K,)), dma((1,)),
            dma((K, Y - 1)), dma((K, Y - 1)),
            dma((K, Z - 1)), dma((K, Z - 1)),
            dma((K, Z - 1)), dma((K, Z - 1)),
            dma((K, Y - 1)), dma((K, Y - 1)),
            dma((K,)), dma((K,)), dma((K,)),
        ],
        compiler_params=pltpu.CompilerParams(
            collective_id=0, has_side_effects=True, vmem_limit_bytes=64 * 2**20
        ),
        name="layers",
    )(lengths, tokens, cotangent, proj, attn_bias, up_bias, gains, shifts, *own)


def unpack_kernel(reduced, attn_g, out_g, up_g, down_g, bias_g, gain_g, shift_g, upb_g, rows, wide, few, ls, ss):
    moves = []
    for layer in (1, 0):
        at = (1 - layer) * LAYER_ROWS
        for i in range(2):
            for half in range(2):
                moves.append((at, [(0, D, down_g.at[layer, pl.ds(i * D, D), pl.ds(half * W, W)])]))
                at += D
            for half in range(2):
                moves.append((at, [(0, D, up_g.at[layer, :, pl.ds((2 * i + half) * W, W)])]))
                at += D
        moves.append((at, [(h * W, W, out_g.at[layer, :, pl.ds(h * W, W)]) for h in range(2)]))
        at += D
        for j in range(3):
            moves.append((at, [(0, D, attn_g.at[layer, j])]))
            at += D

    def load(n):
        at = moves[n][0]
        return pltpu.make_async_copy(reduced.at[pl.ds(at, D)], rows.at[pl.ds(at, D)], ls.at[n])

    def stores(n):
        at = moves[n][0]
        return [
            pltpu.make_async_copy(wide.at[pl.ds(at + r, size)], dst, ss.at[n, q])
            for q, (r, size, dst) in enumerate(moves[n][1])
        ]

    last = pltpu.make_async_copy(reduced.at[pl.ds(2 * LAYER_ROWS, 32)], few, ls.at[len(moves)])
    for n in range(len(moves)):
        load(n).start()
    last.start()
    for n in range(len(moves)):
        load(n).wait()
        at = moves[n][0]

        def body(i, carry):
            r = pl.ds(al(at + i * 96), 96)
            wide[r, :] = rows[r, :].astype(f32)
            return carry

        lax.fori_loop(0, D // 96, body, 0)
        for c in stores(n):
            c.start()
    last.wait()
    v = few[...].astype(f32)
    for layer in range(2):
        r = (1 - layer) * 13
        gain_g[layer] = v[r : r + 2]
        shift_g[layer] = v[r + 2 : r + 6]
        bias_g[layer] = v[r + 6 : r + 9]
        for i in range(4):
            upb_g[layer : layer + 1, i * W : (i + 1) * W] = v[r + 9 + i : r + 10 + i]
    for n in range(len(moves)):
        for c in stores(n):
            c.wait()


def unpack(reduced):
    shape = jax.ShapeDtypeStruct
    hbm, vspec = pl.BlockSpec(memory_space=pltpu.HBM), pl.BlockSpec(memory_space=pltpu.VMEM)
    vm, dma = pltpu.VMEM, pltpu.SemaphoreType.DMA
    return pl.pallas_call(
        unpack_kernel,
        out_shape=[
            shape((2, 3, D, W), f32), shape((2, W, D), f32), shape((2, D, FF // 2), f32),
            shape((2, FF // 2, D), f32), shape((2, 3, W), f32), shape((2, 2, W), f32),
            shape((2, 4, W), f32), shape((2, FF // 2), f32),
        ],
        in_specs=[hbm],
        out_specs=[hbm] * 4 + [vspec] * 4,
        scratch_shapes=[
            vm((2 * LAYER_ROWS, W), bf), vm((2 * LAYER_ROWS, W), f32), vm((32, W), bf),
            dma((25,)), dma((24, 2)),
        ],
        compiler_params=pltpu.CompilerParams(vmem_limit_bytes=60 * 2**20),
        name="unpack",
    )(reduced)


def on_device(
    dp, tokens, cotangent, lengths, random_proj, attn_weight, attn_bias, out_weight, norm_gains,
    biases, up_weight, up_bias, down_weight,
):
    own = (attn_weight.reshape(2, 3 * D, W), out_weight, up_weight, down_weight)
    result = run_main(
        dp, lengths, tokens, cotangent, jnp.swapaxes(random_proj, 2, 3), attn_bias, up_bias, norm_gains, biases, own
    )
    stack_out, tokens_grad, reduced = result[:3]
    attn_g, out_g, up_g, down_g, bias_g, gain_g, shift_g, upb_g = unpack(reduced)
    return (
        stack_out, tokens_grad, attn_g, bias_g, out_g, gain_g, shift_g, up_g, upb_g, down_g,
    )


def solution(mesh):
    return jax.shard_map(
        functools.partial(on_device, mesh.shape["dp"]),
        mesh=mesh,
        in_specs=(
            P(("dp", "mp"), None), P(("dp", "mp"), None), P(("dp", "mp"), None), P(),
            P(None, None, None, "mp"), P(None, None, "mp"), P(None, "mp", None), P(), P(),
            P(None, None, "mp"), P(None, "mp"), P(None, "mp", None),
        ),
        out_specs=(
            P(("dp", "mp"), None), P(("dp", "mp"), None), P(None, None, None, "mp"),
            P(None, None, "mp"), P(None, "mp", None), P(None, None, "mp"), P(None, None, "mp"),
            P(None, None, "mp"), P(None, "mp"), P(None, "mp", None),
        ),
        check_vma=False,
    )
```

```python
import functools
import math

import jax
import jax.numpy as jnp
from jax import lax
from jax.experimental import pallas as pl
from jax.experimental.pallas import tpu as pltpu
from jax.sharding import PartitionSpec as P

MESH = pl.DeviceIdType.MESH
f32, bf = jnp.float32, jnp.bfloat16
TOK, D, HEADS, HD, FEATS = 256, 768, 12, 64, 32
W = D // 2
FF = 4 * D
RING = 4 * D
LAYER_ROWS = 12 * D
LAG = 2
STAGES = [1, 4, 6, 8, 10, 12]
CUTS = (((1,), (1,), (2, 2), (2, 2)), ((1,), (1,), (2, 2), (2, 4, 4)))
Z = 4


def rdma(src, dst, send, recv, dev):
    return pltpu.make_async_remote_copy(
        src_ref=src, dst_ref=dst, send_sem=send, recv_sem=recv, device_id=dev, device_id_type=MESH
    )


def dot_nn(a, b):
    return jnp.dot(a, b, preferred_element_type=f32)


def dot_nt(a, b):
    return lax.dot_general(a, b, (((1,), (1,)), ((), ())), preferred_element_type=f32)


def dot_tn(a, b):
    return lax.dot_general(a, b, (((0,), (0,)), ((), ())), preferred_element_type=f32)


def split_two(v):
    high = v.astype(bf)
    return high, (v - high.astype(f32)).astype(bf)


def al(v, m=16):
    return pl.multiple_of(v, m)


def chunks_of(dp):
    step = D if dp <= 16 else 16 * dp
    out = [(at, step) for at in range(0, 2 * LAYER_ROWS, step)]
    if step > 16 * dp:
        at, size = out.pop()
        out += [(r, 16 * dp) for r in range(at, at + size, 16 * dp)]
    return out + [(2 * LAYER_ROWS, 16 * dp)]


def gather_groups(rows):
    groups = []
    for layer in range(2):
        for t in range(4):
            at = 0
            for share in CUTS[layer][t]:
                size = rows[t] // share
                third = size // 3
                groups.append(
                    [(layer, t, at, third, False), (layer, t, at + third, size - third, True)]
                )
                at += size
    return groups


def rows_loop(body, tile, init=0):
    def step(i, carry):
        return body(pl.ds(al(i * tile, tile), tile), carry)

    return lax.fori_loop(0, TOK // tile, step, init)


def fold(v):
    return jnp.sum(v.reshape(v.shape[0] // 8, 8, v.shape[1]), axis=0)


def main_kernel(
    dp, chunks,
    lengths, tokens, cotangent, proj, attn_bias, up_bias, gains, shifts,
    own_a, own_o, own_u, own_d,
    stack_out, tokens_grad, reduced, oth_a, oth_o, oth_u, oth_d, cland, xland,
    own_small, oth_small, wq, wo, wu, wd,
    X, mid, nrm, sec, qf, kf, sq, sk, vv, rden, ctx, act, dgl,
    pbh, pbl, mask, cosv, sinv, t0, t1, t2, gn, gq, trans, sm,
    stage, acc, xsend, cslot, xslot, ybuf, zbuf,
    gs, gr, wsem, lsem, cs, cr, cl, xs, xr, xl, ys, yr, zs, zr, bs, br, as_, ar, es, er, os,
):
    Y = dp // (2 * Z)
    d, x = lax.axis_index("dp"), lax.axis_index("mp")
    core = d % 2
    yy, zz = (d // 2) % Y, d // (2 * Y)
    ys_peer = [(yy + i) % Y for i in range(1, Y)]
    zs_peer = [(zz + i) % Z for i in range(1, Z)]
    to_x = (d, 1 - x)
    to_core = (d + 1 - 2 * core, x)
    to_y = [((zz * Y + p) * 2 + core, x) for p in ys_peer]
    to_z = [((p * Y + yy) * 2 + core, x) for p in zs_peer]
    peers = [to_core, to_x] + to_y + to_z
    barrier = pltpu.get_barrier_semaphore()
    own_small[...] = jnp.zeros_like(own_small)
    for layer in range(2):
        own_small[3 * layer : 3 * layer + 3, :] = attn_bias[layer].astype(f32)
        row = up_bias[layer : layer + 1, :].astype(f32)
        for i in range(4):
            own_small[6 + 4 * layer + i : 7 + 4 * layer + i, :] = row[:, i * W : (i + 1) * W]
    for peer in peers:
        pl.semaphore_signal(barrier, inc=1, device_id=peer, device_id_type=MESH)
    pl.semaphore_wait(barrier, len(peers))

    own = (own_a, own_o, own_u, own_d)
    oth = (oth_a, oth_o, oth_u, oth_d)
    y1, z1 = (d // 2) % 2, (d // 4) % 2
    gather_y = (d + 2 - 4 * y1, x)
    gather_z = (d + 4 - 8 * z1, x)
    groups = gather_groups([r.shape[1] for r in own])
    G = len(groups)

    def hop(u, i, stage_):
        layer, t, first, rows, wide = groups[u][i]
        piece = rows // (8 if wide else 4)
        base = first + core * (rows // 2)
        src = oth[t]
        if stage_ == 0:
            start = base + (z1 * 2 + y1 if wide else y1) * piece
            size, dev, src = piece, to_x, own[t]
        elif stage_ == 1:
            start = base + (z1 * 2 + y1 if wide else y1) * piece
            size, dev = piece, gather_y
        elif stage_ == 2:
            start, size, dev = base + z1 * 2 * piece, 2 * piece, gather_z
        else:
            start, size, dev = base, rows // 2, to_core
        return rdma(
            src.at[layer, pl.ds(al(start), size)],
            oth[t].at[layer, pl.ds(al(start), size)],
            gs.at[u, 4 * i + stage_],
            gr.at[u, 4 * i + stage_],
            dev,
        )

    small_copy = rdma(own_small, oth_small, gs.at[G, 0], gr.at[G, 0], to_x)
    small_copy.start()
    for u in range(G):
        hop(u, 0, 0).start()
        hop(u, 1, 0).start()
    pumped = [0]

    def pump(count):
        for step in range(pumped[0], min(pumped[0] + count, G + 2 * LAG)):
            u = step - 2 * LAG
            if 0 <= u < G:
                hop(u, 1, 2).wait_recv()
                hop(u, 1, 3).start()
            u = step - LAG
            if 0 <= u < G:
                hop(u, 1, 1).wait_recv()
                hop(u, 1, 2).start()
                hop(u, 0, 1).wait_recv()
                hop(u, 0, 3).start()
            u = step
            if u < G:
                hop(u, 1, 0).wait_recv()
                hop(u, 1, 1).start()
                hop(u, 0, 0).wait_recv()
                hop(u, 0, 1).start()
            pumped[0] = step + 1

    def weight_copies(t, layer, mine):
        src = (own if mine else oth)[t].at[layer]
        m = 0 if mine else 1
        sem = wsem.at[t, m]
        if t == 0:
            return [
                pltpu.make_async_copy(
                    src.at[pl.ds(j * D, D)], wq.at[j, :, pl.ds(m * W, W)], wsem.at[4 + j, m]
                )
                for j in range(3)
            ]
        if t == 1:
            return [pltpu.make_async_copy(src, wo.at[pl.ds(m * W, W)], sem)]
        if t == 2:
            return [pltpu.make_async_copy(src, wu.at[:, pl.ds(m * (FF // 2), FF // 2)], sem)]
        return [pltpu.make_async_copy(src, wd.at[pl.ds(m * (FF // 2), FF // 2)], sem)]

    def load_weight(t, layer, mine):
        for c in weight_copies(t, layer, mine):
            c.start()

    def wait_weight(t, layer, halves=(True, False)):
        for mine in halves:
            for c in weight_copies(t, layer, mine):
                c.wait()

    def late_copies(u):
        layer, t, first, size, _ = groups[u][0]
        size += groups[u][1][3]
        src = oth[t].at[layer, pl.ds(first, size)]
        if t == 0:
            return weight_copies(0, layer, False)
        if t == 1:
            return weight_copies(1, layer, False)
        if t == 2:
            dst = wu.at[pl.ds(first, size), pl.ds(FF // 2, FF // 2)]
        else:
            dst = wd.at[pl.ds(FF // 2 + first, size)]
        return [pltpu.make_async_copy(src, dst, lsem.at[u])]

    def late_groups(t, layer, parts):
        found = [u for u in range(G) if groups[u][0][:2] == (layer, t)]
        return found if parts is None else [found[p] for p in parts]

    def arrived(t, layer, parts=None):
        for u in late_groups(t, layer, parts):
            hop(u, 0, 3).wait_recv()
            hop(u, 1, 3).wait_recv()
            for c in late_copies(u):
                c.start()

    def wait_late(t, layer, parts=None):
        for u in late_groups(t, layer, parts):
            for c in late_copies(u):
                c.wait()

    K = len(chunks)
    slot_rows = max(size for _, size in chunks) // 2

    def sizes(k):
        at, rows = chunks[k]
        return at, rows, rows // 2, rows // 2 // Y, rows // 2 // Y // Z

    def core_copy(k):
        at, rows, half, _, _ = sizes(k)
        return rdma(
            stage.at[:, pl.ds(al(at % RING + (1 - core) * half), half)],
            cland.at[:, pl.ds(at // 2, half)],
            cs.at[k], cr.at[k], to_core,
        )

    def core_load(k):
        at, rows, half, _, _ = sizes(k)
        return pltpu.make_async_copy(
            cland.at[:, pl.ds(at // 2, half)], cslot.at[:, pl.ds(0, half)], cl.at[0]
        )

    def x_copy(k):
        at, rows, half, _, _ = sizes(k)
        return rdma(
            xsend.at[k % 4, pl.ds(0, half)], xland.at[pl.ds(at // 2, half)], xs.at[k], xr.at[k], to_x
        )

    def x_load(k):
        at, rows, half, _, _ = sizes(k)
        return pltpu.make_async_copy(
            xland.at[pl.ds(at // 2, half)], xslot.at[pl.ds(0, half)], xl.at[0]
        )

    def y_copy(k, i):
        at, rows, half, quarter, _ = sizes(k)
        base = at // (2 * Y) * (Y - 1)
        return rdma(
            acc.at[pl.ds(al(at // 2 + ys_peer[i] * quarter), quarter)],
            ybuf.at[pl.ds(base + i * quarter, quarter)],
            ys.at[k, i], yr.at[k, i], to_y[i],
        )

    def z_copy(k, i):
        at, rows, half, quarter, piece = sizes(k)
        base = at // (2 * Y * Z) * (Z - 1)
        return rdma(
            acc.at[pl.ds(al(at // 2 + yy * quarter + zs_peer[i] * piece), piece)],
            zbuf.at[pl.ds(base + i * piece, piece)],
            zs.at[k, i], zr.at[k, i], to_z[i],
        )

    def mine_rows(k):
        at, rows, half, quarter, piece = sizes(k)
        return (
            pl.ds(al(at // 2 + yy * quarter + zz * piece), piece),
            pl.ds(al(at + core * half + yy * quarter + zz * piece), piece),
        )

    def own_copy(k):
        a, b = mine_rows(k)
        return pltpu.make_async_copy(acc.at[a], reduced.at[b], os.at[k])

    def zb_copy(k, i):
        a, b = mine_rows(k)
        return rdma(acc.at[a], reduced.at[b], bs.at[k, i], br.at[k, i], to_z[i])

    def yb_copy(k, i):
        at, rows, half, quarter, piece = sizes(k)
        r = pl.ds(al(at + core * half + yy * quarter), quarter)
        return rdma(reduced.at[r], reduced.at[r], as_.at[k, i], ar.at[k, i], to_y[i])

    def cb_copy(k):
        at, rows, half, quarter, piece = sizes(k)
        r = pl.ds(al(at + core * half), half)
        return rdma(reduced.at[r], reduced.at[r], es.at[k], er.at[k], to_core)

    def add_rows(total, dst, dst_at, srcs):
        tile = 16
        for size in (128, 96, 64, 48, 32):
            if total % size == 0:
                tile = size
                break

        def body(i, carry):
            r0 = i * tile
            v = None
            for ref, at in srcs:
                part = ref[pl.ds(al(at + r0), tile)].astype(f32)
                v = part if v is None else v + part
            dst[pl.ds(al(dst_at + r0), tile)] = v.astype(bf)
            return carry

        lax.fori_loop(0, total // tile, body, 0)

    def s1(k):
        at, rows, half, quarter, piece = sizes(k)
        core_copy(k).wait_recv()
        core_load(k).start()
        if k >= 4:
            x_copy(k - 4).wait_send()
        core_load(k).wait()
        here = at % RING + core * half
        add_rows(half, xsend.at[k % 4], 0, [(stage.at[1], here), (cslot.at[1], 0)])
        x_copy(k).start()
        add_rows(half, acc, at // 2, [(stage.at[0], here), (cslot.at[0], 0)])

    def s2(k):
        at, rows, half, quarter, piece = sizes(k)
        x_copy(k).wait_recv()
        x_load(k).start()
        x_load(k).wait()
        add_rows(half, acc, at // 2, [(acc, at // 2), (xslot, 0)])
        for i in range(Y - 1):
            y_copy(k, i).start()

    def s3(k):
        at, rows, half, quarter, piece = sizes(k)
        base = at // (2 * Y) * (Y - 1)
        for i in range(Y - 1):
            y_copy(k, i).wait_recv()
        here = at // 2 + yy * quarter
        add_rows(quarter, acc, here, [(acc, here)] + [(ybuf, base + i * quarter) for i in range(Y - 1)])
        for i in range(Z - 1):
            z_copy(k, i).start()

    def s4(k):
        at, rows, half, quarter, piece = sizes(k)
        base = at // (2 * Y * Z) * (Z - 1)
        for i in range(Z - 1):
            z_copy(k, i).wait_recv()
        here = at // 2 + yy * quarter + zz * piece
        add_rows(piece, acc, here, [(acc, here)] + [(zbuf, base + i * piece) for i in range(Z - 1)])
        own_copy(k).start()
        for i in range(Z - 1):
            zb_copy(k, i).start()

    def s5(k):
        own_copy(k).wait()
        for i in range(Z - 1):
            zb_copy(k, i).wait_recv()
        for i in range(Y - 1):
            yb_copy(k, i).start()

    def s6(k):
        for i in range(Y - 1):
            yb_copy(k, i).wait_recv()
        cb_copy(k).start()

    ticked = [0]
    settled = [0]

    def settle(k):
        while settled[0] <= k:
            s1(settled[0])
            core_copy(settled[0]).wait_send()
            settled[0] += 1

    def tick():
        t = ticked[0]
        ticked[0] += 1
        for fn, off in reversed(list(zip([s2, s3, s4, s5, s6], STAGES[1:]))):
            if 0 <= t - off < K:
                fn(t - off)
        if 0 <= t - STAGES[0] < K:
            settle(t - STAGES[0])

    made = [0]

    def reserve(start, size):
        assert all(settled[0] > k for k in range(K) if chunks[k][0] < start + size - RING)

    def produced(upto):
        made[0] = upto
        while ticked[0] < K and chunks[ticked[0]][0] + chunks[ticked[0]][1] <= upto:
            core_copy(ticked[0]).start()
            tick()

    for t in range(4):
        load_weight(t, 0, True)
    row_i = lax.broadcasted_iota(jnp.int32, (TOK, 128), 0)
    lane = lax.broadcasted_iota(jnp.int32, (TOK, 128), 1)
    lane_row = lax.broadcasted_iota(jnp.int32, (1, 128), 1)
    seg_r = jnp.zeros((TOK, 1), jnp.int32)
    seg_c = jnp.zeros((1, TOK), jnp.int32)
    begin = jnp.zeros((TOK, 128), jnp.int32)
    r1 = lax.broadcasted_iota(jnp.int32, (TOK, 1), 0)
    c1 = lax.broadcasted_iota(jnp.int32, (1, TOK), 1)
    finish = jnp.int32(0)
    for i in range(8):
        size = lengths[0, i]
        finish = finish + size
        seg_r = seg_r + jnp.where(r1 >= finish, 1, 0)
        seg_c = seg_c + jnp.where(c1 >= finish, 1, 0)
        begin = begin + jnp.where(row_i >= finish, size, 0)
    mask[...] = jnp.where(seg_r == seg_c, 1.0, 0.0).astype(f32)
    place = (row_i - begin).astype(f32)
    freq = jnp.exp((lane % (HD // 2)).astype(f32) * (-2.0 * math.log(10000.0) / HD))
    angle = place * freq
    low_half = (lane % HD) < (HD // 2)
    cosv[...] = jnp.cos(angle)
    sn = jnp.sin(angle)
    sinv[...] = jnp.where(low_half, -sn, sn)
    low_row = (lane_row % HD) < (HD // 2)
    four = [jnp.where(lane_row // FEATS == i, 1.0, 0.0).astype(bf) for i in range(4)]
    two = [jnp.where(lane_row // HD == i, 1.0, 0.0).astype(f32) for i in range(2)]

    block_row = lax.broadcasted_iota(jnp.int32, (128, 256), 0) // FEATS
    block_col = lax.broadcasted_iota(jnp.int32, (128, 256), 1) // HD
    diag = jnp.where(block_row == block_col, HD ** -0.25, 0.0).astype(f32)
    for layer in range(2):
        for g in range(3):
            pieces = []
            for i in range(4):
                h = 4 * g + i
                first = x if h < 6 else 1 - x
                pieces.append(proj[layer, first * (HEADS // 2) + h % (HEADS // 2)])
            p = jnp.concatenate(pieces, axis=0)
            p = jnp.concatenate([p] * 4, axis=1) * diag
            hi, lo = split_two(p)
            pbh[layer, g] = hi
            pbl[layer, g] = lo

    def swap(u):
        return jnp.where(low_row, pltpu.roll(u, 96, 1), pltpu.roll(u, 32, 1))

    def col128(at):
        return pl.ds(at, 128)

    def up_bias_row(layer, m, i):
        src = own_small if m == 0 else oth_small
        r = 6 + 4 * layer + 2 * i
        return jnp.concatenate([src[r : r + 1, :], src[r + 1 : r + 2, :]], axis=1)

    def gain(layer, i):
        return gains[layer].astype(f32)[i : i + 1, :]

    def shift(layer, i):
        return shifts[layer].astype(f32)[i : i + 1, :]

    def norm_into(src, layer, i, dst):
        g, b = gain(layer, i), shift(layer, 2 * i)

        def body(rows, carry):
            v = src[layer, rows, :]
            c = v - jnp.mean(v, axis=-1, keepdims=True)
            r = lax.rsqrt(jnp.mean(c * c, axis=-1, keepdims=True) + 1e-05)
            dst[layer, rows, :] = (c * r * g + b).astype(bf)
            return carry

        rows_loop(body, 32)

    def project(layer, m):
        src = own_small if m == 0 else oth_small
        cols = pl.ds(m * W, W)
        for j, dst in enumerate((t0, t1, vv.at[layer])):
            row = 3 * layer + j
            dst[:, cols] = (dot_nn(nrm[layer], wq[j, :, cols]) + src[row : row + 1, :]).astype(dst.dtype)

    def feature(src, layer, g, feat, sig):
        parts = []
        for p in range(2):
            u = src[:, col128(256 * g + 128 * p)]
            parts.append(u * cosv[...] + swap(u) * sinv[...])
        hi, lo = split_two(jnp.concatenate(parts, axis=1))
        z = dot_nt(hi, pbh[layer, g]) + dot_nt(lo, pbh[layer, g]) + dot_nt(hi, pbl[layer, g])
        f = jnp.maximum(z, 0.0) + jnp.log1p(jnp.exp(-jnp.abs(z)))
        feat[layer, :, col128(128 * g)] = f.astype(bf)
        sig[layer, :, col128(128 * g)] = jnp.exp(z - f)

    def scores(layer, g, i):
        q = qf[layer, :, col128(128 * g)] * four[i]
        return (dot_nt(q, kf[layer, :, col128(128 * g)]) * mask[...]).astype(bf)

    def attention(layer, g):
        feature(t0, layer, g, qf, sq)
        feature(t1, layer, g, kf, sk)
        ones = jnp.ones((TOK, 128), bf)
        for p in range(2):
            cols = col128(256 * g + 128 * p)
            right = jnp.concatenate([vv[layer, :, cols], ones], axis=1)
            a = dot_nn(scores(layer, g, 2 * p), right)
            b = dot_nn(scores(layer, g, 2 * p + 1), right)
            first = lane_row < HD
            num = jnp.where(first, a[:, :128], b[:, :128])
            den = jnp.where(first, a[:, 128:], b[:, 128:])
            r = 1.0 / den
            rden[layer, :, cols] = r
            ctx[layer, :, cols] = num * r

    def out_project(layer):
        mid[layer] = X[layer] + dot_nn(ctx[layer].astype(bf), wo[...]) + shift(layer, 1)
        norm_into(mid, layer, 1, sec)

    def feed(layer, m, i):
        cols = pl.ds(m * (FF // 2) + i * D, D)
        t0[...] = dot_nn(sec[layer], wu[:, cols])
        b = up_bias_row(layer, m, i)

        def body(rows, carry):
            h = t0[rows, :] + b
            phi = 0.5 + 0.5 * lax.erf(h * (2.0 ** -0.5))
            act[layer, rows, cols] = (h * phi).astype(bf)
            dgl[layer, rows, cols] = (
                phi + h * (jnp.exp(-0.5 * h * h) * ((2.0 * math.pi) ** -0.5))
            ).astype(bf)
            return carry

        rows_loop(body, 16)
        part = dot_nn(act[layer, :, cols], wd[cols, :])
        if (m, i) == (0, 0):
            t2[...] = part + mid[layer] + shift(layer, 3)
        else:
            t2[...] += part

    def put(m, row, v):
        stage[m, pl.ds(row % RING, v.shape[0]), :] = v.astype(bf)

    def early_down(m):
        trans[2 * m] = act[1, :, pl.ds(m * (FF // 2), D)].T
        for half in range(2):
            put(m, half * D, dot_nn(trans[2 * m], gq[0, :, half * W : (half + 1) * W]))

    X[0] = tokens[...].astype(f32)
    norm_into(X, 0, 0, nrm)
    wait_weight(0, 0, (True,))
    pump(1)
    project(0, 0)
    pump(1)
    attention(0, 0)
    pump(4)
    arrived(0, 0)
    small_copy.wait()
    wait_late(0, 0)
    project(0, 1)
    load_weight(0, 1, True)
    pump(1)
    attention(0, 1)
    attention(0, 2)
    arrived(1, 0)
    pump(1)
    wait_weight(1, 0, (True,))
    wait_late(1, 0)
    out_project(0)
    load_weight(1, 1, True)
    pump(1)
    arrived(2, 0)
    wait_weight(2, 0, (True,))
    wait_weight(3, 0, (True,))
    feed(0, 0, 0)
    pump(1)
    feed(0, 0, 1)
    arrived(3, 0, (0,))
    wait_late(2, 0)
    wait_late(3, 0, (0,))
    pump(1)
    feed(0, 1, 0)
    arrived(3, 0, (1,))
    pump(1)
    wait_late(3, 0, (1,))
    feed(0, 1, 1)
    load_weight(2, 1, True)
    load_weight(3, 1, True)
    arrived(0, 1)
    X[1] = t2[...]
    norm_into(X, 1, 0, nrm)
    pump(1)
    arrived(1, 1)
    wait_weight(0, 1, (True,))
    wait_late(0, 1)
    project(1, 0)
    attention(1, 0)
    pump(1)
    project(1, 1)
    attention(1, 1)
    pump(1)
    attention(1, 2)
    wait_weight(1, 1, (True,))
    wait_late(1, 1)
    out_project(1)
    pump(1)
    wait_weight(2, 1, (True,))
    wait_weight(3, 1, (True,))
    feed(1, 0, 0)
    pump(1)
    arrived(2, 1)
    arrived(3, 1, (0,))
    feed(1, 0, 1)
    gn[...] = cotangent[...].astype(f32)
    gq[0] = cotangent[...]
    trans[1] = sec[1].T
    early_down(0)
    wait_late(2, 1)
    wait_late(3, 1, (0,))
    feed(1, 1, 0)
    early_down(1)
    produced(D)
    arrived(3, 1, (1, 2))
    wait_late(3, 1, (1, 2))
    feed(1, 1, 1)
    stack_out[...] = t2[...].astype(bf)

    sm[...] = jnp.zeros_like(sm)

    def full_row(row, v):
        first, second = v[:, :W], v[:, W:]
        sm[0, row : row + 1, :] = jnp.where(x == 0, first, second)
        sm[1, row : row + 1, :] = jnp.where(x == 0, second, first)

    def norm_back(layer, i, src, up, base, dst, base_row):
        g = gain(layer, i)
        zero = jnp.zeros((8, D), f32)

        def body(rows, carry):
            v = src[layer, rows, :]
            u = up[rows, :]
            c = v - jnp.mean(v, axis=-1, keepdims=True)
            r = lax.rsqrt(jnp.mean(c * c, axis=-1, keepdims=True) + 1e-05)
            hat = c * r
            dh = u * g
            dv = r * (
                dh
                - jnp.mean(dh, axis=-1, keepdims=True)
                - hat * jnp.mean(dh * hat, axis=-1, keepdims=True)
            )
            dst[rows, :] = base[rows, :] + dv
            return (carry[0] + fold(u * hat), carry[1] + fold(u))

        a, b = rows_loop(body, 32, (zero, zero))
        full_row(base_row + i, jnp.sum(a, axis=0, keepdims=True))
        full_row(base_row + 2 + 2 * i, jnp.sum(b, axis=0, keepdims=True))

    def column_sum(v):
        return jnp.sum(v.astype(f32), axis=0, keepdims=True)

    produced(2 * D)
    for layer in (1, 0):
        row0 = (1 - layer) * LAYER_ROWS
        small_row = (1 - layer) * 13
        if layer == 0:
            wait_weight(3, 0)
            wait_weight(2, 0)
        fg = gq.at[0]
        if layer == 0:
            fg[...] = gn[...].astype(bf)
        full_row(small_row + 5, column_sum(gn[...].astype(bf)))
        st = trans.at[1]
        if layer == 0:
            st[...] = sec[layer].T
        for i in range(2):
            at = row0 + i * RING
            for half in range(0 if at else 2, 2):
                reserve(at + half * D, D)
                for m in range(2):
                    if half == 0:
                        cols = pl.ds(m * (FF // 2) + i * D, D)
                        trans[2 * m] = act[layer, :, cols].T
                    put(m, at + half * D, dot_nn(trans[2 * m], fg[:, half * W : (half + 1) * W]))
                produced(at + (half + 1) * D)
            reserve(at + 2 * D, 2 * D)
            for m in range(2):
                cols = pl.ds(m * (FF // 2) + i * D, D)
                hg = gq.at[1]
                hg[...] = (dot_nt(fg[...], wd[cols, :]) * dgl[layer, :, cols].astype(f32)).astype(bf)
                for half in range(2):
                    put(m, at + (2 + half) * D, dot_nn(st[...], hg[:, half * W : (half + 1) * W]))
                part = dot_nt(hg[...], wu[:, cols])
                if (i, m) == (0, 0):
                    t0[...] = part
                else:
                    t0[...] += part
                s = column_sum(hg[...])
                sm[m, small_row + 9 + 2 * i : small_row + 10 + 2 * i, :] = s[:, :W]
                sm[m, small_row + 10 + 2 * i : small_row + 11 + 2 * i, :] = s[:, W:]
            produced(at + 4 * D)
        if layer == 1:
            load_weight(3, 0, True)
            load_weight(3, 0, False)
            load_weight(2, 0, True)
            load_weight(2, 0, False)
        norm_back(layer, 1, mid, t0, gn, t1, small_row)
        ag = gq.at[0]
        ag[...] = t1[...].astype(bf)
        full_row(small_row + 3, column_sum(t1[...].astype(bf)))
        if layer == 0:
            wait_weight(1, 0)
        at = row0 + 2 * RING
        trans[0] = ctx[layer].astype(bf).T
        reserve(at, D)
        for m in range(2):
            for half in range(2):
                put(
                    m, at + half * W,
                    dot_nn(trans[0, m * W : (m + 1) * W, :], ag[:, half * W : (half + 1) * W]),
                )
        produced(at + D)
        t0[...] = dot_nt(ag[...], wo[...])
        if layer == 1:
            load_weight(1, 0, True)
            load_weight(1, 0, False)
        trans[0] = nrm[layer].T
        for g in range(3):
            lanes = col128(128 * g)
            kg, qg = kf[layer, :, lanes], qf[layer, :, lanes]
            dq = dk = None
            for p in range(2):
                cols = col128(256 * g + 128 * p)
                dn = t0[:, cols] * rden[layer, :, cols]
                cx = ctx[layer, :, cols]
                vp = vv[layer, :, cols]
                dv = None
                for h in range(2):
                    i = 2 * p + h
                    a = scores(layer, g, i)
                    dn_i = (dn * two[h]).astype(bf)
                    dden = jnp.sum(dn_i.astype(f32) * cx, axis=1, keepdims=True)
                    da = ((dot_nt(dn_i, vp) - dden) * mask[...]).astype(bf)
                    v1 = dot_tn(a, dn_i)
                    q1 = dot_nn(da, kg * four[i])
                    k1 = dot_tn(da, qg * four[i])
                    dv = v1 if dv is None else dv + v1
                    dq = q1 if dq is None else dq + q1
                    dk = k1 if dk is None else dk + k1
                gq[2, :, cols] = dv.astype(bf)
            for slot, dz, sig in ((0, dq, sq), (1, dk, sk)):
                hi, lo = split_two(dz * sig[layer, :, lanes])
                dr = dot_nn(hi, pbh[layer, g]) + dot_nn(lo, pbh[layer, g]) + dot_nn(hi, pbl[layer, g])
                for p in range(2):
                    u = dr[:, 128 * p : 128 * p + 128]
                    gq[slot, :, col128(256 * g + 128 * p)] = (
                        u * cosv[...] - swap(u) * sinv[...]
                    ).astype(bf)
        if layer == 0:
            wait_weight(0, 0)
        at = row0 + 2 * RING + D
        for j in range(3):
            reserve(at + j * D, D)
            for m in range(2):
                put(m, at + j * D, dot_nn(trans[0], gq[j, :, m * W : (m + 1) * W]))
            part = dot_nt(gq[j], wq[j])
            if j == 0:
                t0[...] = part
            else:
                t0[...] += part
            s = column_sum(gq[j])
            sm[0, small_row + 6 + j : small_row + 7 + j, :] = s[:, :W]
            sm[1, small_row + 6 + j : small_row + 7 + j, :] = s[:, W:]
            produced(at + (j + 1) * D)
        if layer == 1:
            load_weight(0, 0, True)
            load_weight(0, 0, False)
        norm_back(layer, 0, X, t0, t1, gn if layer else tokens_grad, small_row)

    at = 2 * LAYER_ROWS
    rows = 16 * dp
    reserve(at, rows)
    stage[:, pl.ds(at % RING, rows), :] = jnp.zeros((2, rows, W), bf)
    for m in range(2):
        put(m, at, sm[m])
    produced(at + rows)
    while ticked[0] < K + STAGES[-1]:
        tick()
    for k in range(K):
        cb_copy(k).wait_recv()
        cb_copy(k).wait_send()
        if k >= K - 4:
            x_copy(k).wait_send()
        for i in range(Y - 1):
            y_copy(k, i).wait_send()
            yb_copy(k, i).wait_send()
        for i in range(Z - 1):
            z_copy(k, i).wait_send()
            zb_copy(k, i).wait_send()
    for u in range(G):
        for i in range(2):
            for s in range(4):
                if s != 2 or i:
                    hop(u, i, s).wait_send()


def run_main(dp, lengths, tokens, cotangent, proj, attn_bias, up_bias, gains, shifts, own):
    chunks = chunks_of(dp)
    K = len(chunks)
    Y = dp // (2 * Z)
    rows = sum(size for _, size in chunks)
    slot = max(size for _, size in chunks) // 2
    G = sum(len(c) for layer in CUTS for c in layer)
    dma, vm = pltpu.SemaphoreType.DMA, pltpu.VMEM
    hbm, vspec = pl.BlockSpec(memory_space=pltpu.HBM), pl.BlockSpec(memory_space=pltpu.VMEM)
    shape = jax.ShapeDtypeStruct
    out_shape = [shape((TOK, D), bf), shape((TOK, D), f32), shape((rows, W), bf)]
    out_shape += [shape(a.shape, a.dtype) for a in own]
    out_shape += [shape((2, rows // 2, W), bf), shape((rows // 2, W), bf)]
    return pl.pallas_call(
        functools.partial(main_kernel, dp, chunks),
        out_shape=out_shape,
        in_specs=[pl.BlockSpec(memory_space=pltpu.SMEM)] + [vspec] * 7 + [hbm] * 4,
        out_specs=[vspec, vspec] + [hbm] * 7,
        scratch_shapes=[
            vm((16, W), f32), vm((16, W), f32),
            vm((3, D, D), bf), vm((D, D), bf), vm((D, FF), bf), vm((FF, D), bf),
            vm((2, TOK, D), f32), vm((2, TOK, D), f32), vm((2, TOK, D), bf), vm((2, TOK, D), bf),
            vm((2, TOK, W), bf), vm((2, TOK, W), bf), vm((2, TOK, W), f32), vm((2, TOK, W), f32),
            vm((2, TOK, D), bf), vm((2, TOK, D), f32), vm((2, TOK, D), f32),
            vm((2, TOK, FF), bf), vm((2, TOK, FF), bf),
            vm((2, 3, 128, 256), bf), vm((2, 3, 128, 256), bf),
            vm((TOK, TOK), f32), vm((TOK, 128), f32), vm((TOK, 128), f32),
            vm((TOK, D), f32), vm((TOK, D), f32), vm((TOK, D), f32), vm((TOK, D), f32),
            vm((3, TOK, D), bf), vm((3, D, TOK), bf), vm((2, 32, W), f32),
            vm((2, RING, W), bf), vm((rows // 2, W), bf),
            vm((4, slot, W), bf), vm((2, slot, W), bf), vm((slot, W), bf),
            vm((rows // (2 * Y) * (Y - 1), W), bf), vm((rows // (2 * Y * Z) * (Z - 1), W), bf),
            dma((G + 1, 8)), dma((G + 1, 8)), dma((7, 2)), dma((G,)),
            dma((K,)), dma((K,)), dma((1,)), dma((K,)), dma((K,)), dma((1,)),
            dma((K, Y - 1)), dma((K, Y - 1)),
            dma((K, Z - 1)), dma((K, Z - 1)),
            dma((K, Z - 1)), dma((K, Z - 1)),
            dma((K, Y - 1)), dma((K, Y - 1)),
            dma((K,)), dma((K,)), dma((K,)),
        ],
        compiler_params=pltpu.CompilerParams(
            collective_id=0, has_side_effects=True, vmem_limit_bytes=64 * 2**20
        ),
        name="layers",
    )(lengths, tokens, cotangent, proj, attn_bias, up_bias, gains, shifts, *own)


def unpack_kernel(reduced, attn_g, out_g, up_g, down_g, bias_g, gain_g, shift_g, upb_g, rows, wide, few, ls, ss):
    moves = []
    for layer in (1, 0):
        at = (1 - layer) * LAYER_ROWS
        for i in range(2):
            for half in range(2):
                moves.append((at, [(0, D, down_g.at[layer, pl.ds(i * D, D), pl.ds(half * W, W)])]))
                at += D
            for half in range(2):
                moves.append((at, [(0, D, up_g.at[layer, :, pl.ds((2 * i + half) * W, W)])]))
                at += D
        moves.append((at, [(h * W, W, out_g.at[layer, :, pl.ds(h * W, W)]) for h in range(2)]))
        at += D
        for j in range(3):
            moves.append((at, [(0, D, attn_g.at[layer, j])]))
            at += D

    def load(n):
        at = moves[n][0]
        return pltpu.make_async_copy(reduced.at[pl.ds(at, D)], rows.at[pl.ds(at, D)], ls.at[n])

    def stores(n):
        at = moves[n][0]
        return [
            pltpu.make_async_copy(wide.at[pl.ds(at + r, size)], dst, ss.at[n, q])
            for q, (r, size, dst) in enumerate(moves[n][1])
        ]

    last = pltpu.make_async_copy(reduced.at[pl.ds(2 * LAYER_ROWS, 32)], few, ls.at[len(moves)])
    for n in range(len(moves)):
        load(n).start()
    last.start()
    for n in range(len(moves)):
        load(n).wait()
        at = moves[n][0]

        def body(i, carry):
            r = pl.ds(al(at + i * 96), 96)
            wide[r, :] = rows[r, :].astype(f32)
            return carry

        lax.fori_loop(0, D // 96, body, 0)
        for c in stores(n):
            c.start()
    last.wait()
    v = few[...].astype(f32)
    for layer in range(2):
        r = (1 - layer) * 13
        gain_g[layer] = v[r : r + 2]
        shift_g[layer] = v[r + 2 : r + 6]
        bias_g[layer] = v[r + 6 : r + 9]
        for i in range(4):
            upb_g[layer : layer + 1, i * W : (i + 1) * W] = v[r + 9 + i : r + 10 + i]
    for n in range(len(moves)):
        for c in stores(n):
            c.wait()


def unpack(reduced):
    shape = jax.ShapeDtypeStruct
    hbm, vspec = pl.BlockSpec(memory_space=pltpu.HBM), pl.BlockSpec(memory_space=pltpu.VMEM)
    vm, dma = pltpu.VMEM, pltpu.SemaphoreType.DMA
    return pl.pallas_call(
        unpack_kernel,
        out_shape=[
            shape((2, 3, D, W), f32), shape((2, W, D), f32), shape((2, D, FF // 2), f32),
            shape((2, FF // 2, D), f32), shape((2, 3, W), f32), shape((2, 2, W), f32),
            shape((2, 4, W), f32), shape((2, FF // 2), f32),
        ],
        in_specs=[hbm],
        out_specs=[hbm] * 4 + [vspec] * 4,
        scratch_shapes=[
            vm((2 * LAYER_ROWS, W), bf), vm((2 * LAYER_ROWS, W), f32), vm((32, W), bf),
            dma((25,)), dma((24, 2)),
        ],
        compiler_params=pltpu.CompilerParams(vmem_limit_bytes=60 * 2**20),
        name="unpack",
    )(reduced)


def on_device(
    dp, tokens, cotangent, lengths, random_proj, attn_weight, attn_bias, out_weight, norm_gains,
    biases, up_weight, up_bias, down_weight,
):
    own = (attn_weight.reshape(2, 3 * D, W), out_weight, up_weight, down_weight)
    result = run_main(
        dp, lengths, tokens, cotangent, jnp.swapaxes(random_proj, 2, 3), attn_bias, up_bias, norm_gains, biases, own
    )
    stack_out, tokens_grad, reduced = result[:3]
    attn_g, out_g, up_g, down_g, bias_g, gain_g, shift_g, upb_g = unpack(reduced)
    return (
        stack_out, tokens_grad, attn_g, bias_g, out_g, gain_g, shift_g, up_g, upb_g, down_g,
    )


def solution(mesh):
    return jax.shard_map(
        functools.partial(on_device, mesh.shape["dp"]),
        mesh=mesh,
        in_specs=(
            P(("dp", "mp"), None), P(("dp", "mp"), None), P(("dp", "mp"), None), P(),
            P(None, None, None, "mp"), P(None, None, "mp"), P(None, "mp", None), P(), P(),
            P(None, None, "mp"), P(None, "mp"), P(None, "mp", None),
        ),
        out_specs=(
            P(("dp", "mp"), None), P(("dp", "mp"), None), P(None, None, None, "mp"),
            P(None, None, "mp"), P(None, "mp", None), P(None, None, "mp"), P(None, None, "mp"),
            P(None, None, "mp"), P(None, "mp"), P(None, "mp", None),
        ),
        check_vma=False,
    )
```

```python
import functools
import math

import jax
import jax.numpy as jnp
from jax import lax
from jax.experimental import pallas as pl
from jax.experimental.pallas import tpu as pltpu
from jax.sharding import PartitionSpec as P

MESH = pl.DeviceIdType.MESH
f32, bf = jnp.float32, jnp.bfloat16
TOK, D, HEADS, HD, FEATS = 256, 768, 12, 64, 32
W = D // 2
FF = 4 * D
RING = 4 * D
LAYER_ROWS = 12 * D
LAG = 2
STAGES = [1, 4, 6, 8, 10, 12]
CUTS = (((1,), (1,), (2, 2), (2, 2)), ((1,), (1,), (2, 2), (2, 4, 4)))
Z = 4


def rdma(src, dst, send, recv, dev):
    return pltpu.make_async_remote_copy(
        src_ref=src, dst_ref=dst, send_sem=send, recv_sem=recv, device_id=dev, device_id_type=MESH
    )


def dot_nn(a, b):
    return jnp.dot(a, b, preferred_element_type=f32)


def dot_nt(a, b):
    return lax.dot_general(a, b, (((1,), (1,)), ((), ())), preferred_element_type=f32)


def dot_tn(a, b):
    return lax.dot_general(a, b, (((0,), (0,)), ((), ())), preferred_element_type=f32)


def split_two(v):
    high = v.astype(bf)
    return high, (v - high.astype(f32)).astype(bf)


def al(v, m=16):
    return pl.multiple_of(v, m)


def chunks_of(dp):
    step = D if dp <= 16 else 16 * dp
    out = [(at, step) for at in range(0, 2 * LAYER_ROWS, step)]
    if step > 16 * dp:
        at, size = out.pop()
        out += [(r, 16 * dp) for r in range(at, at + size, 16 * dp)]
    return out + [(2 * LAYER_ROWS, 16 * dp)]


def gather_groups(rows):
    groups = []
    for layer in range(2):
        for t in range(4):
            at = 0
            for share in CUTS[layer][t]:
                size = rows[t] // share
                third = size // 3
                groups.append(
                    [(layer, t, at, third, False), (layer, t, at + third, size - third, True)]
                )
                at += size
    return groups


def rows_loop(body, tile, init=0):
    def step(i, carry):
        return body(pl.ds(al(i * tile, tile), tile), carry)

    return lax.fori_loop(0, TOK // tile, step, init)


def fold(v):
    return jnp.sum(v.reshape(v.shape[0] // 8, 8, v.shape[1]), axis=0)


def main_kernel(
    dp, chunks,
    lengths, tokens, cotangent, proj, attn_bias, up_bias, gains, shifts,
    own_a, own_o, own_u, own_d,
    stack_out, tokens_grad, reduced, oth_a, oth_o, oth_u, oth_d, cland, xland,
    own_small, oth_small, wq, wo, wu, wd,
    X, mid, nrm, sec, qf, kf, sq, sk, vv, rden, ctx, act, dgl,
    pbh, pbl, mask, cosv, sinv, t0, t1, t2, gn, gq, trans, sm,
    stage, acc, xsend, cslot, xslot, ybuf, zbuf,
    gs, gr, wsem, lsem, cs, cr, cl, xs, xr, xl, ys, yr, zs, zr, bs, br, as_, ar, es, er, os,
):
    Y = dp // (2 * Z)
    d, x = lax.axis_index("dp"), lax.axis_index("mp")
    core = d % 2
    yy, zz = (d // 2) % Y, d // (2 * Y)
    ys_peer = [(yy + i) % Y for i in range(1, Y)]
    zs_peer = [(zz + i) % Z for i in range(1, Z)]
    to_x = (d, 1 - x)
    to_core = (d + 1 - 2 * core, x)
    to_y = [((zz * Y + p) * 2 + core, x) for p in ys_peer]
    to_z = [((p * Y + yy) * 2 + core, x) for p in zs_peer]
    peers = [to_core, to_x] + to_y + to_z
    barrier = pltpu.get_barrier_semaphore()
    own_small[...] = jnp.zeros_like(own_small)
    for layer in range(2):
        own_small[3 * layer : 3 * layer + 3, :] = attn_bias[layer].astype(f32)
        row = up_bias[layer : layer + 1, :].astype(f32)
        for i in range(4):
            own_small[6 + 4 * layer + i : 7 + 4 * layer + i, :] = row[:, i * W : (i + 1) * W]
    for peer in peers:
        pl.semaphore_signal(barrier, inc=1, device_id=peer, device_id_type=MESH)
    pl.semaphore_wait(barrier, len(peers))

    own = (own_a, own_o, own_u, own_d)
    oth = (oth_a, oth_o, oth_u, oth_d)
    y1, z1 = (d // 2) % 2, (d // 4) % 2
    gather_y = (d + 2 - 4 * y1, x)
    gather_z = (d + 4 - 8 * z1, x)
    groups = gather_groups([r.shape[1] for r in own])
    G = len(groups)

    def hop(u, i, stage_):
        layer, t, first, rows, wide = groups[u][i]
        piece = rows // (8 if wide else 4)
        base = first + core * (rows // 2)
        src = oth[t]
        if stage_ == 0:
            start = base + (z1 * 2 + y1 if wide else y1) * piece
            size, dev, src = piece, to_x, own[t]
        elif stage_ == 1:
            start = base + (z1 * 2 + y1 if wide else y1) * piece
            size, dev = piece, gather_y
        elif stage_ == 2:
            start, size, dev = base + z1 * 2 * piece, 2 * piece, gather_z
        else:
            start, size, dev = base, rows // 2, to_core
        return rdma(
            src.at[layer, pl.ds(al(start), size)],
            oth[t].at[layer, pl.ds(al(start), size)],
            gs.at[u, 4 * i + stage_],
            gr.at[u, 4 * i + stage_],
            dev,
        )

    small_copy = rdma(own_small, oth_small, gs.at[G, 0], gr.at[G, 0], to_x)
    small_copy.start()
    for u in range(G):
        hop(u, 0, 0).start()
        hop(u, 1, 0).start()
    pumped = [0]

    def pump(count):
        for step in range(pumped[0], min(pumped[0] + count, G + 2 * LAG)):
            u = step - 2 * LAG
            if 0 <= u < G:
                hop(u, 1, 2).wait_recv()
                hop(u, 1, 3).start()
            u = step - LAG
            if 0 <= u < G:
                hop(u, 1, 1).wait_recv()
                hop(u, 1, 2).start()
                hop(u, 0, 1).wait_recv()
                hop(u, 0, 3).start()
            u = step
            if u < G:
                hop(u, 1, 0).wait_recv()
                hop(u, 1, 1).start()
                hop(u, 0, 0).wait_recv()
                hop(u, 0, 1).start()
            pumped[0] = step + 1

    def weight_copies(t, layer, mine):
        src = (own if mine else oth)[t].at[layer]
        m = 0 if mine else 1
        sem = wsem.at[t, m]
        if t == 0:
            return [
                pltpu.make_async_copy(
                    src.at[pl.ds(j * D, D)], wq.at[j, :, pl.ds(m * W, W)], wsem.at[4 + j, m]
                )
                for j in range(3)
            ]
        if t == 1:
            return [pltpu.make_async_copy(src, wo.at[pl.ds(m * W, W)], sem)]
        if t == 2:
            return [pltpu.make_async_copy(src, wu.at[:, pl.ds(m * (FF // 2), FF // 2)], sem)]
        return [pltpu.make_async_copy(src, wd.at[pl.ds(m * (FF // 2), FF // 2)], sem)]

    def load_weight(t, layer, mine):
        for c in weight_copies(t, layer, mine):
            c.start()

    def wait_weight(t, layer, halves=(True, False)):
        for mine in halves:
            for c in weight_copies(t, layer, mine):
                c.wait()

    def late_copies(u):
        layer, t, first, size, _ = groups[u][0]
        size += groups[u][1][3]
        src = oth[t].at[layer, pl.ds(first, size)]
        if t == 0:
            return weight_copies(0, layer, False)
        if t == 1:
            return weight_copies(1, layer, False)
        if t == 2:
            dst = wu.at[pl.ds(first, size), pl.ds(FF // 2, FF // 2)]
        else:
            dst = wd.at[pl.ds(FF // 2 + first, size)]
        return [pltpu.make_async_copy(src, dst, lsem.at[u])]

    def late_groups(t, layer, parts):
        found = [u for u in range(G) if groups[u][0][:2] == (layer, t)]
        return found if parts is None else [found[p] for p in parts]

    def arrived(t, layer, parts=None):
        for u in late_groups(t, layer, parts):
            hop(u, 0, 3).wait_recv()
            hop(u, 1, 3).wait_recv()
            for c in late_copies(u):
                c.start()

    def wait_late(t, layer, parts=None):
        for u in late_groups(t, layer, parts):
            for c in late_copies(u):
                c.wait()

    K = len(chunks)
    slot_rows = max(size for _, size in chunks) // 2

    def sizes(k):
        at, rows = chunks[k]
        return at, rows, rows // 2, rows // 2 // Y, rows // 2 // Y // Z

    def core_copy(k):
        at, rows, half, _, _ = sizes(k)
        return rdma(
            stage.at[:, pl.ds(al(at % RING + (1 - core) * half), half)],
            cland.at[:, pl.ds(at // 2, half)],
            cs.at[k], cr.at[k], to_core,
        )

    def core_load(k):
        at, rows, half, _, _ = sizes(k)
        return pltpu.make_async_copy(
            cland.at[:, pl.ds(at // 2, half)], cslot.at[:, pl.ds(0, half)], cl.at[0]
        )

    def x_copy(k):
        at, rows, half, _, _ = sizes(k)
        return rdma(
            xsend.at[k % 4, pl.ds(0, half)], xland.at[pl.ds(at // 2, half)], xs.at[k], xr.at[k], to_x
        )

    def x_load(k):
        at, rows, half, _, _ = sizes(k)
        return pltpu.make_async_copy(
            xland.at[pl.ds(at // 2, half)], xslot.at[pl.ds(0, half)], xl.at[0]
        )

    def y_copy(k, i):
        at, rows, half, quarter, _ = sizes(k)
        base = at // (2 * Y) * (Y - 1)
        return rdma(
            acc.at[pl.ds(al(at // 2 + ys_peer[i] * quarter), quarter)],
            ybuf.at[pl.ds(base + i * quarter, quarter)],
            ys.at[k, i], yr.at[k, i], to_y[i],
        )

    def z_copy(k, i):
        at, rows, half, quarter, piece = sizes(k)
        base = at // (2 * Y * Z) * (Z - 1)
        return rdma(
            acc.at[pl.ds(al(at // 2 + yy * quarter + zs_peer[i] * piece), piece)],
            zbuf.at[pl.ds(base + i * piece, piece)],
            zs.at[k, i], zr.at[k, i], to_z[i],
        )

    def mine_rows(k):
        at, rows, half, quarter, piece = sizes(k)
        return (
            pl.ds(al(at // 2 + yy * quarter + zz * piece), piece),
            pl.ds(al(at + core * half + yy * quarter + zz * piece), piece),
        )

    def own_copy(k):
        a, b = mine_rows(k)
        return pltpu.make_async_copy(acc.at[a], reduced.at[b], os.at[k])

    def zb_copy(k, i):
        a, b = mine_rows(k)
        return rdma(acc.at[a], reduced.at[b], bs.at[k, i], br.at[k, i], to_z[i])

    def yb_copy(k, i):
        at, rows, half, quarter, piece = sizes(k)
        r = pl.ds(al(at + core * half + yy * quarter), quarter)
        return rdma(reduced.at[r], reduced.at[r], as_.at[k, i], ar.at[k, i], to_y[i])

    def cb_copy(k):
        at, rows, half, quarter, piece = sizes(k)
        r = pl.ds(al(at + core * half), half)
        return rdma(reduced.at[r], reduced.at[r], es.at[k], er.at[k], to_core)

    def add_rows(total, dst, dst_at, srcs):
        tile = 16
        for size in (128, 96, 64, 48, 32):
            if total % size == 0:
                tile = size
                break

        def body(i, carry):
            r0 = i * tile
            v = None
            for ref, at in srcs:
                part = ref[pl.ds(al(at + r0), tile)].astype(f32)
                v = part if v is None else v + part
            dst[pl.ds(al(dst_at + r0), tile)] = v.astype(bf)
            return carry

        lax.fori_loop(0, total // tile, body, 0)

    def s1(k):
        at, rows, half, quarter, piece = sizes(k)
        if k >= 4:
            x_copy(k - 4).wait_send()
        core_load(k).wait()
        here = at % RING + core * half
        add_rows(half, xsend.at[k % 4], 0, [(stage.at[1], here), (cslot.at[1], 0)])
        x_copy(k).start()
        add_rows(half, acc, at // 2, [(stage.at[0], here), (cslot.at[0], 0)])

    def s2(k):
        at, rows, half, quarter, piece = sizes(k)
        x_copy(k).wait_recv()
        x_load(k).start()
        x_load(k).wait()
        add_rows(half, acc, at // 2, [(acc, at // 2), (xslot, 0)])
        for i in range(Y - 1):
            y_copy(k, i).start()

    def s3(k):
        at, rows, half, quarter, piece = sizes(k)
        base = at // (2 * Y) * (Y - 1)
        for i in range(Y - 1):
            y_copy(k, i).wait_recv()
        here = at // 2 + yy * quarter
        add_rows(quarter, acc, here, [(acc, here)] + [(ybuf, base + i * quarter) for i in range(Y - 1)])
        for i in range(Z - 1):
            z_copy(k, i).start()

    def s4(k):
        at, rows, half, quarter, piece = sizes(k)
        base = at // (2 * Y * Z) * (Z - 1)
        for i in range(Z - 1):
            z_copy(k, i).wait_recv()
        here = at // 2 + yy * quarter + zz * piece
        add_rows(piece, acc, here, [(acc, here)] + [(zbuf, base + i * piece) for i in range(Z - 1)])
        own_copy(k).start()
        for i in range(Z - 1):
            zb_copy(k, i).start()

    def s5(k):
        own_copy(k).wait()
        for i in range(Z - 1):
            zb_copy(k, i).wait_recv()
        for i in range(Y - 1):
            yb_copy(k, i).start()

    def s6(k):
        for i in range(Y - 1):
            yb_copy(k, i).wait_recv()
        cb_copy(k).start()

    ticked = [0]
    settled = [0]

    def settle(k):
        while settled[0] <= k:
            s1(settled[0])
            core_copy(settled[0]).wait_send()
            settled[0] += 1

    def tick():
        t = ticked[0]
        ticked[0] += 1
        due = t - STAGES[0]
        if 0 <= due < K:
            assert settled[0] == due
            core_copy(due).wait_recv()
            core_load(due).start()
        for fn, off in reversed(list(zip([s2, s3, s4, s5, s6], STAGES[1:]))):
            if 0 <= t - off < K:
                fn(t - off)
        if 0 <= t - STAGES[0] < K:
            settle(t - STAGES[0])

    made = [0]

    def reserve(start, size):
        assert all(settled[0] > k for k in range(K) if chunks[k][0] < start + size - RING)

    def produced(upto):
        made[0] = upto
        while ticked[0] < K and chunks[ticked[0]][0] + chunks[ticked[0]][1] <= upto:
            core_copy(ticked[0]).start()
            tick()

    for t in range(4):
        load_weight(t, 0, True)
    row_i = lax.broadcasted_iota(jnp.int32, (TOK, 128), 0)
    lane = lax.broadcasted_iota(jnp.int32, (TOK, 128), 1)
    lane_row = lax.broadcasted_iota(jnp.int32, (1, 128), 1)
    seg_r = jnp.zeros((TOK, 1), jnp.int32)
    seg_c = jnp.zeros((1, TOK), jnp.int32)
    begin = jnp.zeros((TOK, 128), jnp.int32)
    r1 = lax.broadcasted_iota(jnp.int32, (TOK, 1), 0)
    c1 = lax.broadcasted_iota(jnp.int32, (1, TOK), 1)
    finish = jnp.int32(0)
    for i in range(8):
        size = lengths[0, i]
        finish = finish + size
        seg_r = seg_r + jnp.where(r1 >= finish, 1, 0)
        seg_c = seg_c + jnp.where(c1 >= finish, 1, 0)
        begin = begin + jnp.where(row_i >= finish, size, 0)
    mask[...] = jnp.where(seg_r == seg_c, 1.0, 0.0).astype(f32)
    place = (row_i - begin).astype(f32)
    freq = jnp.exp((lane % (HD // 2)).astype(f32) * (-2.0 * math.log(10000.0) / HD))
    angle = place * freq
    low_half = (lane % HD) < (HD // 2)
    cosv[...] = jnp.cos(angle)
    sn = jnp.sin(angle)
    sinv[...] = jnp.where(low_half, -sn, sn)
    low_row = (lane_row % HD) < (HD // 2)
    four = [jnp.where(lane_row // FEATS == i, 1.0, 0.0).astype(bf) for i in range(4)]
    two = [jnp.where(lane_row // HD == i, 1.0, 0.0).astype(f32) for i in range(2)]

    block_row = lax.broadcasted_iota(jnp.int32, (128, 256), 0) // FEATS
    block_col = lax.broadcasted_iota(jnp.int32, (128, 256), 1) // HD
    diag = jnp.where(block_row == block_col, HD ** -0.25, 0.0).astype(f32)
    for layer in range(2):
        for g in range(3):
            pieces = []
            for i in range(4):
                h = 4 * g + i
                first = x if h < 6 else 1 - x
                pieces.append(proj[layer, first * (HEADS // 2) + h % (HEADS // 2)])
            p = jnp.concatenate(pieces, axis=0)
            p = jnp.concatenate([p] * 4, axis=1) * diag
            hi, lo = split_two(p)
            pbh[layer, g] = hi
            pbl[layer, g] = lo

    def swap(u):
        return jnp.where(low_row, pltpu.roll(u, 96, 1), pltpu.roll(u, 32, 1))

    def col128(at):
        return pl.ds(at, 128)

    def up_bias_row(layer, m, i):
        src = own_small if m == 0 else oth_small
        r = 6 + 4 * layer + 2 * i
        return jnp.concatenate([src[r : r + 1, :], src[r + 1 : r + 2, :]], axis=1)

    def gain(layer, i):
        return gains[layer].astype(f32)[i : i + 1, :]

    def shift(layer, i):
        return shifts[layer].astype(f32)[i : i + 1, :]

    def norm_into(src, layer, i, dst):
        g, b = gain(layer, i), shift(layer, 2 * i)

        def body(rows, carry):
            v = src[layer, rows, :]
            c = v - jnp.mean(v, axis=-1, keepdims=True)
            r = lax.rsqrt(jnp.mean(c * c, axis=-1, keepdims=True) + 1e-05)
            dst[layer, rows, :] = (c * r * g + b).astype(bf)
            return carry

        rows_loop(body, 32)

    def project(layer, m):
        src = own_small if m == 0 else oth_small
        cols = pl.ds(m * W, W)
        for j, dst in enumerate((t0, t1, vv.at[layer])):
            row = 3 * layer + j
            dst[:, cols] = (dot_nn(nrm[layer], wq[j, :, cols]) + src[row : row + 1, :]).astype(dst.dtype)

    def feature(src, layer, g, feat, sig):
        parts = []
        for p in range(2):
            u = src[:, col128(256 * g + 128 * p)]
            parts.append(u * cosv[...] + swap(u) * sinv[...])
        hi, lo = split_two(jnp.concatenate(parts, axis=1))
        z = dot_nt(hi, pbh[layer, g]) + dot_nt(lo, pbh[layer, g]) + dot_nt(hi, pbl[layer, g])
        f = jnp.maximum(z, 0.0) + jnp.log1p(jnp.exp(-jnp.abs(z)))
        feat[layer, :, col128(128 * g)] = f.astype(bf)
        sig[layer, :, col128(128 * g)] = jnp.exp(z - f)

    def scores(layer, g, i):
        q = qf[layer, :, col128(128 * g)] * four[i]
        return (dot_nt(q, kf[layer, :, col128(128 * g)]) * mask[...]).astype(bf)

    def attention(layer, g):
        feature(t0, layer, g, qf, sq)
        feature(t1, layer, g, kf, sk)
        ones = jnp.ones((TOK, 128), bf)
        for p in range(2):
            cols = col128(256 * g + 128 * p)
            right = jnp.concatenate([vv[layer, :, cols], ones], axis=1)
            a = dot_nn(scores(layer, g, 2 * p), right)
            b = dot_nn(scores(layer, g, 2 * p + 1), right)
            first = lane_row < HD
            num = jnp.where(first, a[:, :128], b[:, :128])
            den = jnp.where(first, a[:, 128:], b[:, 128:])
            r = 1.0 / den
            rden[layer, :, cols] = r
            ctx[layer, :, cols] = num * r

    def out_project(layer):
        mid[layer] = X[layer] + dot_nn(ctx[layer].astype(bf), wo[...]) + shift(layer, 1)
        norm_into(mid, layer, 1, sec)

    def feed(layer, m, i):
        cols = pl.ds(m * (FF // 2) + i * D, D)
        t0[...] = dot_nn(sec[layer], wu[:, cols])
        b = up_bias_row(layer, m, i)

        def body(rows, carry):
            h = t0[rows, :] + b
            phi = 0.5 + 0.5 * lax.erf(h * (2.0 ** -0.5))
            act[layer, rows, cols] = (h * phi).astype(bf)
            dgl[layer, rows, cols] = (
                phi + h * (jnp.exp(-0.5 * h * h) * ((2.0 * math.pi) ** -0.5))
            ).astype(bf)
            return carry

        rows_loop(body, 16)
        part = dot_nn(act[layer, :, cols], wd[cols, :])
        if (m, i) == (0, 0):
            t2[...] = part + mid[layer] + shift(layer, 3)
        else:
            t2[...] += part

    def put(m, row, v):
        stage[m, pl.ds(row % RING, v.shape[0]), :] = v.astype(bf)

    def early_down(m):
        trans[2 * m] = act[1, :, pl.ds(m * (FF // 2), D)].T
        for half in range(2):
            put(m, half * D, dot_nn(trans[2 * m], gq[0, :, half * W : (half + 1) * W]))

    X[0] = tokens[...].astype(f32)
    norm_into(X, 0, 0, nrm)
    wait_weight(0, 0, (True,))
    pump(1)
    project(0, 0)
    pump(1)
    attention(0, 0)
    pump(4)
    arrived(0, 0)
    small_copy.wait()
    wait_late(0, 0)
    project(0, 1)
    load_weight(0, 1, True)
    pump(1)
    attention(0, 1)
    attention(0, 2)
    arrived(1, 0)
    pump(1)
    wait_weight(1, 0, (True,))
    wait_late(1, 0)
    out_project(0)
    load_weight(1, 1, True)
    pump(1)
    arrived(2, 0)
    wait_weight(2, 0, (True,))
    wait_weight(3, 0, (True,))
    feed(0, 0, 0)
    pump(1)
    feed(0, 0, 1)
    arrived(3, 0, (0,))
    wait_late(2, 0)
    wait_late(3, 0, (0,))
    pump(1)
    feed(0, 1, 0)
    arrived(3, 0, (1,))
    pump(1)
    wait_late(3, 0, (1,))
    feed(0, 1, 1)
    load_weight(2, 1, True)
    load_weight(3, 1, True)
    arrived(0, 1)
    X[1] = t2[...]
    norm_into(X, 1, 0, nrm)
    pump(1)
    arrived(1, 1)
    wait_weight(0, 1, (True,))
    wait_late(0, 1)
    project(1, 0)
    attention(1, 0)
    pump(1)
    project(1, 1)
    attention(1, 1)
    pump(1)
    attention(1, 2)
    wait_weight(1, 1, (True,))
    wait_late(1, 1)
    out_project(1)
    pump(1)
    wait_weight(2, 1, (True,))
    wait_weight(3, 1, (True,))
    feed(1, 0, 0)
    pump(1)
    arrived(2, 1)
    arrived(3, 1, (0,))
    feed(1, 0, 1)
    gn[...] = cotangent[...].astype(f32)
    gq[0] = cotangent[...]
    trans[1] = sec[1].T
    early_down(0)
    wait_late(2, 1)
    wait_late(3, 1, (0,))
    feed(1, 1, 0)
    early_down(1)
    produced(D)
    arrived(3, 1, (1, 2))
    wait_late(3, 1, (1, 2))
    feed(1, 1, 1)
    stack_out[...] = t2[...].astype(bf)

    sm[...] = jnp.zeros_like(sm)

    def full_row(row, v):
        first, second = v[:, :W], v[:, W:]
        sm[0, row : row + 1, :] = jnp.where(x == 0, first, second)
        sm[1, row : row + 1, :] = jnp.where(x == 0, second, first)

    def norm_back(layer, i, src, up, base, dst, base_row):
        g = gain(layer, i)
        zero = jnp.zeros((8, D), f32)

        def body(rows, carry):
            v = src[layer, rows, :]
            u = up[rows, :]
            c = v - jnp.mean(v, axis=-1, keepdims=True)
            r = lax.rsqrt(jnp.mean(c * c, axis=-1, keepdims=True) + 1e-05)
            hat = c * r
            dh = u * g
            dv = r * (
                dh
                - jnp.mean(dh, axis=-1, keepdims=True)
                - hat * jnp.mean(dh * hat, axis=-1, keepdims=True)
            )
            dst[rows, :] = base[rows, :] + dv
            return (carry[0] + fold(u * hat), carry[1] + fold(u))

        a, b = rows_loop(body, 32, (zero, zero))
        full_row(base_row + i, jnp.sum(a, axis=0, keepdims=True))
        full_row(base_row + 2 + 2 * i, jnp.sum(b, axis=0, keepdims=True))

    def column_sum(v):
        return jnp.sum(v.astype(f32), axis=0, keepdims=True)

    produced(2 * D)
    for layer in (1, 0):
        row0 = (1 - layer) * LAYER_ROWS
        small_row = (1 - layer) * 13
        if layer == 0:
            wait_weight(3, 0)
            wait_weight(2, 0)
        fg = gq.at[0]
        if layer == 0:
            fg[...] = gn[...].astype(bf)
        full_row(small_row + 5, column_sum(gn[...].astype(bf)))
        st = trans.at[1]
        if layer == 0:
            st[...] = sec[layer].T
        for i in range(2):
            at = row0 + i * RING
            for half in range(0 if at else 2, 2):
                reserve(at + half * D, D)
                for m in range(2):
                    if half == 0:
                        cols = pl.ds(m * (FF // 2) + i * D, D)
                        trans[2 * m] = act[layer, :, cols].T
                    put(m, at + half * D, dot_nn(trans[2 * m], fg[:, half * W : (half + 1) * W]))
                produced(at + (half + 1) * D)
            reserve(at + 2 * D, 2 * D)
            for m in range(2):
                cols = pl.ds(m * (FF // 2) + i * D, D)
                hg = gq.at[1]
                hg[...] = (dot_nt(fg[...], wd[cols, :]) * dgl[layer, :, cols].astype(f32)).astype(bf)
                for half in range(2):
                    put(m, at + (2 + half) * D, dot_nn(st[...], hg[:, half * W : (half + 1) * W]))
                part = dot_nt(hg[...], wu[:, cols])
                if (i, m) == (0, 0):
                    t0[...] = part
                else:
                    t0[...] += part
                s = column_sum(hg[...])
                sm[m, small_row + 9 + 2 * i : small_row + 10 + 2 * i, :] = s[:, :W]
                sm[m, small_row + 10 + 2 * i : small_row + 11 + 2 * i, :] = s[:, W:]
            produced(at + 4 * D)
        if layer == 1:
            load_weight(3, 0, True)
            load_weight(3, 0, False)
            load_weight(2, 0, True)
            load_weight(2, 0, False)
        norm_back(layer, 1, mid, t0, gn, t1, small_row)
        ag = gq.at[0]
        ag[...] = t1[...].astype(bf)
        full_row(small_row + 3, column_sum(t1[...].astype(bf)))
        if layer == 0:
            wait_weight(1, 0)
        at = row0 + 2 * RING
        trans[0] = ctx[layer].astype(bf).T
        reserve(at, D)
        for m in range(2):
            for half in range(2):
                put(
                    m, at + half * W,
                    dot_nn(trans[0, m * W : (m + 1) * W, :], ag[:, half * W : (half + 1) * W]),
                )
        produced(at + D)
        t0[...] = dot_nt(ag[...], wo[...])
        if layer == 1:
            load_weight(1, 0, True)
            load_weight(1, 0, False)
        trans[0] = nrm[layer].T
        for g in range(3):
            lanes = col128(128 * g)
            kg, qg = kf[layer, :, lanes], qf[layer, :, lanes]
            dq = dk = None
            for p in range(2):
                cols = col128(256 * g + 128 * p)
                dn = t0[:, cols] * rden[layer, :, cols]
                cx = ctx[layer, :, cols]
                vp = vv[layer, :, cols]
                dv = None
                for h in range(2):
                    i = 2 * p + h
                    a = scores(layer, g, i)
                    dn_i = (dn * two[h]).astype(bf)
                    dden = jnp.sum(dn_i.astype(f32) * cx, axis=1, keepdims=True)
                    da = ((dot_nt(dn_i, vp) - dden) * mask[...]).astype(bf)
                    v1 = dot_tn(a, dn_i)
                    q1 = dot_nn(da, kg * four[i])
                    k1 = dot_tn(da, qg * four[i])
                    dv = v1 if dv is None else dv + v1
                    dq = q1 if dq is None else dq + q1
                    dk = k1 if dk is None else dk + k1
                gq[2, :, cols] = dv.astype(bf)
            for slot, dz, sig in ((0, dq, sq), (1, dk, sk)):
                hi, lo = split_two(dz * sig[layer, :, lanes])
                dr = dot_nn(hi, pbh[layer, g]) + dot_nn(lo, pbh[layer, g]) + dot_nn(hi, pbl[layer, g])
                for p in range(2):
                    u = dr[:, 128 * p : 128 * p + 128]
                    gq[slot, :, col128(256 * g + 128 * p)] = (
                        u * cosv[...] - swap(u) * sinv[...]
                    ).astype(bf)
        if layer == 0:
            wait_weight(0, 0)
        at = row0 + 2 * RING + D
        for j in range(3):
            reserve(at + j * D, D)
            for m in range(2):
                put(m, at + j * D, dot_nn(trans[0], gq[j, :, m * W : (m + 1) * W]))
            part = dot_nt(gq[j], wq[j])
            if j == 0:
                t0[...] = part
            else:
                t0[...] += part
            s = column_sum(gq[j])
            sm[0, small_row + 6 + j : small_row + 7 + j, :] = s[:, :W]
            sm[1, small_row + 6 + j : small_row + 7 + j, :] = s[:, W:]
            produced(at + (j + 1) * D)
        if layer == 1:
            load_weight(0, 0, True)
            load_weight(0, 0, False)
        norm_back(layer, 0, X, t0, t1, gn if layer else tokens_grad, small_row)

    at = 2 * LAYER_ROWS
    rows = 16 * dp
    reserve(at, rows)
    stage[:, pl.ds(at % RING, rows), :] = jnp.zeros((2, rows, W), bf)
    for m in range(2):
        put(m, at, sm[m])
    produced(at + rows)
    while ticked[0] < K + STAGES[-1]:
        tick()
    for k in range(K):
        cb_copy(k).wait_recv()
        cb_copy(k).wait_send()
        if k >= K - 4:
            x_copy(k).wait_send()
        for i in range(Y - 1):
            y_copy(k, i).wait_send()
            yb_copy(k, i).wait_send()
        for i in range(Z - 1):
            z_copy(k, i).wait_send()
            zb_copy(k, i).wait_send()
    for u in range(G):
        for i in range(2):
            for s in range(4):
                if s != 2 or i:
                    hop(u, i, s).wait_send()


def run_main(dp, lengths, tokens, cotangent, proj, attn_bias, up_bias, gains, shifts, own):
    chunks = chunks_of(dp)
    K = len(chunks)
    Y = dp // (2 * Z)
    rows = sum(size for _, size in chunks)
    slot = max(size for _, size in chunks) // 2
    G = sum(len(c) for layer in CUTS for c in layer)
    dma, vm = pltpu.SemaphoreType.DMA, pltpu.VMEM
    hbm, vspec = pl.BlockSpec(memory_space=pltpu.HBM), pl.BlockSpec(memory_space=pltpu.VMEM)
    shape = jax.ShapeDtypeStruct
    out_shape = [shape((TOK, D), bf), shape((TOK, D), f32), shape((rows, W), bf)]
    out_shape += [shape(a.shape, a.dtype) for a in own]
    out_shape += [shape((2, rows // 2, W), bf), shape((rows // 2, W), bf)]
    return pl.pallas_call(
        functools.partial(main_kernel, dp, chunks),
        out_shape=out_shape,
        in_specs=[pl.BlockSpec(memory_space=pltpu.SMEM)] + [vspec] * 7 + [hbm] * 4,
        out_specs=[vspec, vspec] + [hbm] * 7,
        scratch_shapes=[
            vm((16, W), f32), vm((16, W), f32),
            vm((3, D, D), bf), vm((D, D), bf), vm((D, FF), bf), vm((FF, D), bf),
            vm((2, TOK, D), f32), vm((2, TOK, D), f32), vm((2, TOK, D), bf), vm((2, TOK, D), bf),
            vm((2, TOK, W), bf), vm((2, TOK, W), bf), vm((2, TOK, W), f32), vm((2, TOK, W), f32),
            vm((2, TOK, D), bf), vm((2, TOK, D), f32), vm((2, TOK, D), f32),
            vm((2, TOK, FF), bf), vm((2, TOK, FF), bf),
            vm((2, 3, 128, 256), bf), vm((2, 3, 128, 256), bf),
            vm((TOK, TOK), f32), vm((TOK, 128), f32), vm((TOK, 128), f32),
            vm((TOK, D), f32), vm((TOK, D), f32), vm((TOK, D), f32), vm((TOK, D), f32),
            vm((3, TOK, D), bf), vm((3, D, TOK), bf), vm((2, 32, W), f32),
            vm((2, RING, W), bf), vm((rows // 2, W), bf),
            vm((4, slot, W), bf), vm((2, slot, W), bf), vm((slot, W), bf),
            vm((rows // (2 * Y) * (Y - 1), W), bf), vm((rows // (2 * Y * Z) * (Z - 1), W), bf),
            dma((G + 1, 8)), dma((G + 1, 8)), dma((7, 2)), dma((G,)),
            dma((K,)), dma((K,)), dma((1,)), dma((K,)), dma((K,)), dma((1,)),
            dma((K, Y - 1)), dma((K, Y - 1)),
            dma((K, Z - 1)), dma((K, Z - 1)),
            dma((K, Z - 1)), dma((K, Z - 1)),
            dma((K, Y - 1)), dma((K, Y - 1)),
            dma((K,)), dma((K,)), dma((K,)),
        ],
        compiler_params=pltpu.CompilerParams(
            collective_id=0, has_side_effects=True, vmem_limit_bytes=64 * 2**20
        ),
        name="layers",
    )(lengths, tokens, cotangent, proj, attn_bias, up_bias, gains, shifts, *own)


def unpack_kernel(reduced, attn_g, out_g, up_g, down_g, bias_g, gain_g, shift_g, upb_g, rows, wide, few, ls, ss):
    moves = []
    for layer in (1, 0):
        at = (1 - layer) * LAYER_ROWS
        for i in range(2):
            for half in range(2):
                moves.append((at, [(0, D, down_g.at[layer, pl.ds(i * D, D), pl.ds(half * W, W)])]))
                at += D
            for half in range(2):
                moves.append((at, [(0, D, up_g.at[layer, :, pl.ds((2 * i + half) * W, W)])]))
                at += D
        moves.append((at, [(h * W, W, out_g.at[layer, :, pl.ds(h * W, W)]) for h in range(2)]))
        at += D
        for j in range(3):
            moves.append((at, [(0, D, attn_g.at[layer, j])]))
            at += D

    def load(n):
        at = moves[n][0]
        return pltpu.make_async_copy(reduced.at[pl.ds(at, D)], rows.at[pl.ds(at, D)], ls.at[n])

    def stores(n):
        at = moves[n][0]
        return [
            pltpu.make_async_copy(wide.at[pl.ds(at + r, size)], dst, ss.at[n, q])
            for q, (r, size, dst) in enumerate(moves[n][1])
        ]

    last = pltpu.make_async_copy(reduced.at[pl.ds(2 * LAYER_ROWS, 32)], few, ls.at[len(moves)])
    for n in range(len(moves)):
        load(n).start()
    last.start()
    for n in range(len(moves)):
        load(n).wait()
        at = moves[n][0]

        def body(i, carry):
            r = pl.ds(al(at + i * 96), 96)
            wide[r, :] = rows[r, :].astype(f32)
            return carry

        lax.fori_loop(0, D // 96, body, 0)
        for c in stores(n):
            c.start()
    last.wait()
    v = few[...].astype(f32)
    for layer in range(2):
        r = (1 - layer) * 13
        gain_g[layer] = v[r : r + 2]
        shift_g[layer] = v[r + 2 : r + 6]
        bias_g[layer] = v[r + 6 : r + 9]
        for i in range(4):
            upb_g[layer : layer + 1, i * W : (i + 1) * W] = v[r + 9 + i : r + 10 + i]
    for n in range(len(moves)):
        for c in stores(n):
            c.wait()


def unpack(reduced):
    shape = jax.ShapeDtypeStruct
    hbm, vspec = pl.BlockSpec(memory_space=pltpu.HBM), pl.BlockSpec(memory_space=pltpu.VMEM)
    vm, dma = pltpu.VMEM, pltpu.SemaphoreType.DMA
    return pl.pallas_call(
        unpack_kernel,
        out_shape=[
            shape((2, 3, D, W), f32), shape((2, W, D), f32), shape((2, D, FF // 2), f32),
            shape((2, FF // 2, D), f32), shape((2, 3, W), f32), shape((2, 2, W), f32),
            shape((2, 4, W), f32), shape((2, FF // 2), f32),
        ],
        in_specs=[hbm],
        out_specs=[hbm] * 4 + [vspec] * 4,
        scratch_shapes=[
            vm((2 * LAYER_ROWS, W), bf), vm((2 * LAYER_ROWS, W), f32), vm((32, W), bf),
            dma((25,)), dma((24, 2)),
        ],
        compiler_params=pltpu.CompilerParams(vmem_limit_bytes=60 * 2**20),
        name="unpack",
    )(reduced)


def on_device(
    dp, tokens, cotangent, lengths, random_proj, attn_weight, attn_bias, out_weight, norm_gains,
    biases, up_weight, up_bias, down_weight,
):
    own = (attn_weight.reshape(2, 3 * D, W), out_weight, up_weight, down_weight)
    result = run_main(
        dp, lengths, tokens, cotangent, jnp.swapaxes(random_proj, 2, 3), attn_bias, up_bias, norm_gains, biases, own
    )
    stack_out, tokens_grad, reduced = result[:3]
    attn_g, out_g, up_g, down_g, bias_g, gain_g, shift_g, upb_g = unpack(reduced)
    return (
        stack_out, tokens_grad, attn_g, bias_g, out_g, gain_g, shift_g, up_g, upb_g, down_g,
    )


def solution(mesh):
    return jax.shard_map(
        functools.partial(on_device, mesh.shape["dp"]),
        mesh=mesh,
        in_specs=(
            P(("dp", "mp"), None), P(("dp", "mp"), None), P(("dp", "mp"), None), P(),
            P(None, None, None, "mp"), P(None, None, "mp"), P(None, "mp", None), P(), P(),
            P(None, None, "mp"), P(None, "mp"), P(None, "mp", None),
        ),
        out_specs=(
            P(("dp", "mp"), None), P(("dp", "mp"), None), P(None, None, None, "mp"),
            P(None, None, "mp"), P(None, "mp", None), P(None, None, "mp"), P(None, None, "mp"),
            P(None, None, "mp"), P(None, "mp"), P(None, "mp", None),
        ),
        check_vma=False,
    )
```
